256 devices in a mesh: row: 32 (over y_hi, z, core), ch: 8 (over y_lo, x).
Axes of the slice: x: 4, y: 4 (y_hi: 2, y_lo: 2; y = y_hi * 2 + y_lo), z: 8, core: 2. Of those that a mesh axis runs over, the one named last changes fastest.
Arguments:
- pair_act: bfloat16 [512, 512, 128], P('row', 'ch'), may hold values from -240 to 240
- cotangent: bfloat16 [512, 512, 128], P('row', 'ch'), may hold values from -6 to 6
- in_gain: float32 [128], replicated, may hold values from 0.25 to 1.75
- in_bias: float32 [128], replicated, may hold values from -3 to 3
- proj_weight: bfloat16 [128, 640], replicated, may hold values from -0.5 to 0.5
- out_gain: float32 [128], replicated, may hold values from 0.25 to 1.75
- out_bias: float32 [128], replicated, may hold values from -3 to 3
- out_weight: bfloat16 [128, 128], replicated, may hold values from -0.5 to 0.5
Outputs:
- grad_pair: bfloat16 [512, 512, 128], P('row', 'ch')
The draws below stay inside these ranges and needn't reach their ends.
All inputs are finite; a program needn't handle non-finite values.
Results may differ from the reference program's by a relative error of at most 0.0072.
Values may be sent and summed in bfloat16 or wider, within the bound.
A program may use at most 64 MiB of HBM per device.

```python
import math
import jax
import jax.numpy as jnp
from jax import lax

C = 128
N = 512


def draw_pair_act(key, part):
    key = jax.random.fold_in(key, 7)
    noise_key, pair_key, chan_key = jax.random.split(key, 3)
    pair_scale = jnp.exp(jax.random.uniform(pair_key, (N, N, 1), jnp.float32) * math.log(10.0))
    chan_scale = jnp.exp(jax.random.uniform(chan_key, (1, 1, C), jnp.float32) * math.log(4.0))
    noise_field = jnp.clip(jax.random.normal(noise_key, (N, N, C), jnp.float32), -6.0, 6.0)
    return (noise_field * pair_scale * chan_scale).astype(jnp.bfloat16)


def block_levels(rng, dims, cuts, low, high):
    loudness = 1.0
    for position, shards_of in cuts:
        heights = jax.random.uniform(jax.random.fold_in(jax.random.fold_in(rng, 6), position), (shards_of,), jnp.float32, low / len(cuts), high / len(cuts))
        loudness = loudness * jnp.repeat(jnp.exp(heights), dims[position] // shards_of).reshape((-1,) + (1,) * (len(dims) - 1 - position))
    return loudness


def normal_values(key, shape, width, most, pieces=(), kind=jnp.bfloat16):
    drawn = jax.random.normal(key, shape, jnp.float32) * width
    if len(pieces) > 0:
        drawn = block_levels(key, shape, pieces, -0.22, 0.18) * drawn
    return jnp.clip(drawn, min=-most, max=most).astype(kind)


def setup_inputs(seed: int = 0) -> dict:
    arg_keys = jax.random.split(jax.random.key(seed), 9)
    return {
        "pair_act": draw_pair_act(jax.random.fold_in(arg_keys[8], 71), 0),
        "cotangent": normal_values(arg_keys[1], (N, N, C), 1.0, 6.0, ((0, 32), (1, 8))),
        "in_gain": jnp.clip(1.0 + 0.15 * jax.random.normal(arg_keys[2], (C,), jnp.float32), 0.25, 1.75),
        "in_bias": normal_values(arg_keys[3], (C,), 0.5, 3.0, (), jnp.float32),
        "proj_weight": normal_values(arg_keys[4], (C, 5 * C), C ** -0.5, 0.5),
        "out_gain": jnp.clip(1.0 + 0.15 * jax.random.normal(arg_keys[5], (C,), jnp.float32), 0.25, 1.75),
        "out_bias": normal_values(arg_keys[6], (C,), 0.5, 3.0, (), jnp.float32),
        "out_weight": normal_values(arg_keys[7], (C, C), C ** -0.5, 0.5),
    }


EPSILON = 1e-05

def to_half(values):
    return lax.optimization_barrier(values.astype(jnp.bfloat16))

def normalize(values):
    center = lax.optimization_barrier(jnp.mean(values, axis=-1, keepdims=True))
    shifted = values - center
    scale_inv = lax.rsqrt(lax.optimization_barrier(jnp.mean(shifted * shifted, axis=-1, keepdims=True)) + EPSILON)
    return (shifted * scale_inv, scale_inv)

def norm_back(grad_hat, normed, scale_inv):
    first = lax.optimization_barrier(jnp.mean(grad_hat, axis=-1, keepdims=True))
    second = lax.optimization_barrier(jnp.mean(grad_hat * normed, axis=-1, keepdims=True))
    return scale_inv * (grad_hat - first - normed * second)

def reference(pair_act, cotangent, in_gain, in_bias, proj_weight, out_gain, out_bias, out_weight):
    flat = pair_act.astype(jnp.float32).reshape(N * N, C)
    normed, scale_inv = normalize(flat)
    normal_in = (normed * in_gain + in_bias).astype(jnp.bfloat16)
    projected = jnp.dot(normal_in, proj_weight, preferred_element_type=jnp.float32)
    left_val, left_gate, right_val, right_gate, out_logit = jnp.split(projected, 5, axis=-1)
    left_sig = jax.nn.sigmoid(left_gate)
    right_sig = jax.nn.sigmoid(right_gate)
    left_fac = to_half(left_sig * left_val).astype(jnp.float32).reshape(N, N, C)
    right_fac = to_half(right_sig * right_val).astype(jnp.float32).reshape(N, N, C)
    product = jnp.einsum('ikc,jkc->ijc', left_fac, right_fac, precision=lax.Precision.HIGHEST)
    tri_flat = to_half(product).astype(jnp.float32).reshape(N * N, C)
    tri_hat, tri_inv = normalize(tri_flat)
    normal_out = (tri_hat * out_gain + out_bias).astype(jnp.bfloat16)
    mixed = jnp.dot(normal_out, out_weight, preferred_element_type=jnp.float32)
    out_gate = jax.nn.sigmoid(out_logit)
    grad_out = cotangent.astype(jnp.float32).reshape(N * N, C)
    grad_mixed = (grad_out * out_gate).astype(jnp.bfloat16)
    grad_logit = grad_out * mixed * out_gate * (1.0 - out_gate)
    grad_normal = jnp.dot(grad_mixed, out_weight.T, preferred_element_type=jnp.float32)
    grad_tri = to_half(norm_back(grad_normal * out_gain, tri_hat, tri_inv)).astype(jnp.float32).reshape(N, N, C)
    left_sum = jnp.einsum('ijc,jkc->ikc', grad_tri, right_fac, precision=lax.Precision.HIGHEST)
    right_sum = jnp.einsum('ijc,ikc->jkc', grad_tri, left_fac, precision=lax.Precision.HIGHEST)
    grad_left = to_half(left_sum).astype(jnp.float32).reshape(N * N, C)
    grad_right = to_half(right_sum).astype(jnp.float32).reshape(N * N, C)
    grad_proj = jnp.concatenate([grad_left * left_sig, grad_left * left_val * left_sig * (1.0 - left_sig), grad_right * right_sig, grad_right * right_val * right_sig * (1.0 - right_sig), grad_logit], axis=-1).astype(jnp.bfloat16)
    grad_in = jnp.dot(grad_proj, proj_weight.T, preferred_element_type=jnp.float32)
    grad_pair = norm_back(grad_in * in_gain, normed, scale_inv)
    return grad_pair.astype(jnp.bfloat16).reshape(N, N, C)
```

```python
import functools

import jax
import jax.numpy as jnp
from jax import lax
from jax.experimental import pallas as pl
from jax.experimental.pallas import tpu as pltpu
from jax.sharding import PartitionSpec as P

EPSILON = 1e-05
MESH = pl.DeviceIdType.MESH
F32 = jnp.float32
BF16 = jnp.bfloat16
C = 128
N = 512
CHIPS = 128
GROUPS = 8
STRIDE = 37


def nt(a, b):
    return lax.dot_general(a, b, (((1,), (1,)), ((), ())), preferred_element_type=F32)


def nn(a, b):
    return lax.dot_general(a, b, (((1,), (0,)), ((), ())), preferred_element_type=F32)


def swap_halves(a, b):
    axis = a.ndim - 1
    low = lax.broadcasted_iota(jnp.int32, a.shape, axis) < 64
    return (
        jnp.where(low, a, pltpu.roll(b, 64, axis)),
        jnp.where(low, pltpu.roll(a, 64, axis), b),
    )


def column(row_ref):
    return jnp.broadcast_to(row_ref[...], (C, C)).T


def body(
    x_ref, cot_ref, ig_ref, ib_ref, w_ref, og_ref, ob_ref, ow_ref, out_ref,
    wt, owt,
    normed, sinv, left_a, left_b, right_a, right_b, gate, cot_t, grad_acc,
    hid, stage, stage2,
    r_send, r_all, l_send, l_all, t_send, t_recv, g_send, g_all,
    gl_send, gl_recv, gr_send, gr_recv,
    r_f32, r_mat, l_mat, gt_mat, gtt, gr_f32,
    send_sem, recv_sem, core_send, core_recv,
):
    row = lax.axis_index("row")
    ch = lax.axis_index("ch")
    core = lax.rem(row, 2)
    other = 1 - core
    me = (row // 2) * 8 + ch
    partner = (row + 1 - 2 * core, ch)

    def device(chip):
        return ((chip // 8) * 2 + core, lax.rem(chip, 8))

    barrier = pltpu.get_barrier_semaphore()

    def greet(step, carry):
        pl.semaphore_signal(
            barrier, inc=1, device_id=device(lax.rem(me + step, CHIPS)), device_id_type=MESH
        )
        return carry

    pl.semaphore_signal(barrier, inc=1, device_id=partner, device_id_type=MESH)
    lax.fori_loop(1, CHIPS, greet, 0)

    def exchange(which, source, target):
        own = pltpu.make_async_copy(source.at[me], target.at[me], recv_sem.at[which])
        own.start()

        def send(step, carry):
            chip = lax.rem(me + lax.rem(step * STRIDE, CHIPS), CHIPS)
            pltpu.make_async_remote_copy(
                src_ref=source.at[chip],
                dst_ref=target.at[me],
                send_sem=send_sem.at[which],
                recv_sem=recv_sem.at[which],
                device_id=device(chip),
                device_id_type=MESH,
            ).start()
            return carry

        lax.fori_loop(1, CHIPS, send, 0)

    def arrived(which, target):
        pltpu.make_async_copy(target, target, recv_sem.at[which]).wait()

    def sent(which, source):
        most = source.at[pl.ds(0, CHIPS - 1)]
        pltpu.make_async_copy(most, most, send_sem.at[which]).wait()

    def to_partner(which, buffer):
        copy = pltpu.make_async_remote_copy(
            src_ref=buffer.at[core],
            dst_ref=buffer.at[core],
            send_sem=core_send.at[which],
            recv_sem=core_recv.at[which],
            device_id=partner,
            device_id_type=MESH,
        )
        copy.start()

    def from_partner(which, buffer):
        pltpu.make_async_copy(buffer.at[other], buffer.at[other], core_recv.at[which]).wait()

    def to_partner_sent(which, buffer):
        pltpu.make_async_copy(buffer.at[core], buffer.at[core], core_send.at[which]).wait()

    wt[...] = w_ref[...].astype(F32).T.astype(BF16)
    in_gain = column(ig_ref)
    in_bias = column(ib_ref)
    normals = []
    for g in range(GROUPS):
        x = x_ref[pl.ds(g * 128, 128), :].astype(F32).T
        shifted = x - jnp.sum(x, axis=0, keepdims=True) * (1.0 / C)
        scale = lax.rsqrt(jnp.sum(shifted * shifted, axis=0, keepdims=True) * (1.0 / C) + EPSILON)
        hat = shifted * scale
        normed[g] = hat
        sinv[g] = jnp.broadcast_to(scale, (8, 128))
        normal = (hat * in_gain + in_bias).astype(BF16)
        normals.append(normal)
        projected = nn(wt[pl.ds(256, 256), :], normal)
        val, sig = projected[:128], jax.nn.sigmoid(projected[128:])
        factor = sig * val
        right_a[g] = sig
        right_b[g] = factor * (1.0 - sig)
        stage[pl.ds(g, C, stride=8), :] = factor
    r_send[...] = stage[...].reshape(C, 8, 128).astype(BF16)
    pl.semaphore_wait(barrier, CHIPS)
    exchange(0, r_send, r_all.at[core])

    for g in range(GROUPS):
        projected = nn(wt[pl.ds(0, 256), :], normals[g])
        val, sig = projected[:128], jax.nn.sigmoid(projected[128:])
        factor = sig * val
        left_a[g] = sig
        left_b[g] = factor * (1.0 - sig)
        stage2[pl.ds(g, C, stride=8), :] = factor
    l_send[...] = stage2[...].reshape(C, 8, 128).astype(BF16)
    exchange(1, l_send, l_all.at[core])

    owt[...] = ow_ref[...].astype(F32).T.astype(BF16)
    out_gain = column(og_ref)
    mean_h = []
    for g in range(GROUPS):
        out_gate = jax.nn.sigmoid(nn(wt[pl.ds(512, 128), :], normals[g]))
        cotangent = cot_ref[pl.ds(g * 128, 128), :].astype(F32).T
        grad_mixed = cotangent * out_gate
        gate[g] = out_gate
        cot_t[g] = cotangent
        h = nn(ow_ref[...], grad_mixed.astype(BF16)) * out_gain
        hid[pl.ds(g, C, stride=8), :] = h
        mean_h.append(jnp.sum(h, axis=0, keepdims=True) * (1.0 / C))
    mean_h = jnp.concatenate(mean_h, axis=0)

    def place_right(slot):
        tiles = r_all[slot].reshape(16, 8, 8, 128)
        for pair in range(4):
            a = tiles[:, 2 * pair].astype(F32)
            b = tiles[:, 2 * pair + 1].astype(F32)
            even, odd = swap_halves(a, b)
            r_f32[pair, :, pl.ds(16 * slot, 8, stride=2), :] = even
            r_f32[pair, :, pl.ds(16 * slot + 1, 8, stride=2), :] = odd

    def place_pairs(buffer, slot, matrix):
        tiles = buffer[slot].reshape(16, 8, 8, 128)
        for pair in range(4):
            a = tiles[:, 2 * pair].astype(F32).reshape(128, 128)
            b = tiles[:, 2 * pair + 1].astype(F32).reshape(128, 128)
            even, odd = swap_halves(a, b)
            lanes = pl.ds(128 * pair, 128)
            matrix[slot, 0, :, lanes] = even.astype(BF16)
            matrix[slot, 1, :, lanes] = odd.astype(BF16)

    def quarter(matrix, pair):
        return matrix[:, 128 * pair : 128 * pair + 128]

    def pieces(even, odd, buffer):
        for pair in range(4):
            a, b = swap_halves(even(pair), odd(pair))
            a = a.reshape(16, 8, 128).astype(BF16)
            b = b.reshape(16, 8, 128).astype(BF16)
            for q in range(16):
                buffer[8 * q + 2 * pair] = a[q]
                buffer[8 * q + 2 * pair + 1] = b[q]

    arrived(0, r_all.at[core])
    to_partner(0, r_all)
    from_partner(0, r_all)
    place_right(0)
    place_right(1)
    for pair in range(4):
        r_mat[:, pl.ds(128 * pair, 128)] = r_f32[pair].reshape(N, 128).astype(BF16)

    arrived(1, l_all.at[core])
    to_partner(1, l_all)
    place_pairs(l_all, core, l_mat)
    tri = [nt(l_mat[core, parity], r_mat[...]) for parity in range(2)]
    pieces(functools.partial(quarter, tri[0]), functools.partial(quarter, tri[1]), t_send)
    exchange(2, t_send, t_recv)
    from_partner(1, l_all)
    place_pairs(l_all, other, l_mat)

    arrived(2, t_recv)
    tri = t_recv[...].astype(F32)
    mean_tri = jnp.sum(tri, axis=0) * (1.0 / C)
    shifted = tri - mean_tri[None]
    scale_tri = lax.rsqrt(jnp.sum(shifted * shifted, axis=0) * (1.0 / C) + EPSILON)
    h = hid[...].reshape(C, 8, 128)
    second = jnp.sum(h * shifted, axis=0) * (scale_tri * (1.0 / C))
    grad_tri = scale_tri[None] * (h - mean_h[None] - shifted * (scale_tri * second)[None])
    g_send[...] = grad_tri.astype(BF16)
    exchange(3, g_send, g_all.at[core])

    stage[...] = (shifted * scale_tri[None]).reshape(C * 8, 128)
    out_bias = column(ob_ref)
    for g in range(GROUPS):
        hat = stage[pl.ds(g, C, stride=8), :]
        mixed = nn(owt[...], (hat * out_gain + out_bias).astype(BF16))
        out_gate = gate[g]
        grad_logit = cot_t[g] * mixed * out_gate * (1.0 - out_gate)
        grad_acc[g] = nn(w_ref[:, pl.ds(512, 128)], grad_logit.astype(BF16))

    arrived(3, g_all.at[core])
    to_partner(2, g_all)
    place_pairs(g_all, core, gt_mat)
    grad = [nn(gt_mat[core, parity], r_mat[...]) for parity in range(2)]
    pieces(functools.partial(quarter, grad[0]), functools.partial(quarter, grad[1]), gl_send)
    exchange(4, gl_send, gl_recv)
    from_partner(2, g_all)
    place_pairs(g_all, other, gt_mat)
    total = None
    for slot in range(2):
        for parity in range(2):
            gtt[...] = gt_mat[slot, parity].astype(F32).T.reshape(16, 32, 128)
            mine = gtt[:, pl.ds(16 * core, 16), :].reshape(256, 128).astype(BF16)
            part = nn(mine, l_mat[slot, parity])
            total = part if total is None else total + part
    for pair in range(4):
        gr_f32[pair] = quarter(total, pair).reshape(16, 16, 128)
    pieces(
        lambda pair: gr_f32[pair, :, pl.ds(0, 8, stride=2), :].reshape(128, 128),
        lambda pair: gr_f32[pair, :, pl.ds(1, 8, stride=2), :].reshape(128, 128),
        gr_send,
    )
    exchange(5, gr_send, gr_recv)

    arrived(4, gl_recv)
    stage2[...] = gl_recv[...].astype(F32).reshape(C * 8, 128)
    for g in range(GROUPS):
        grad = stage2[pl.ds(g, C, stride=8), :]
        both = jnp.concatenate([grad * left_a[g], grad * left_b[g]], axis=0).astype(BF16)
        grad_acc[g] += nn(w_ref[:, pl.ds(0, 256)], both)

    arrived(5, gr_recv)
    stage[...] = gr_recv[...].astype(F32).reshape(C * 8, 128)
    for g in range(GROUPS):
        grad = stage[pl.ds(g, C, stride=8), :]
        both = jnp.concatenate([grad * right_a[g], grad * right_b[g]], axis=0).astype(BF16)
        full = (grad_acc[g] + nn(w_ref[:, pl.ds(256, 256)], both)) * in_gain
        hat = normed[g]
        first = jnp.sum(full, axis=0, keepdims=True) * (1.0 / C)
        second = jnp.sum(full * hat, axis=0, keepdims=True) * (1.0 / C)
        grad_pair = sinv[g][:1] * (full - first - hat * second)
        out_ref[pl.ds(g * 128, 128), :] = grad_pair.T.astype(BF16)

    for which, source in enumerate((r_send, l_send, t_send, g_send, gl_send, gr_send)):
        sent(which, source)
    for which, buffer in enumerate((r_all, l_all, g_all)):
        to_partner_sent(which, buffer)


def on_device(pair_act, cotangent, in_gain, in_bias, proj_weight, out_gain, out_bias, out_weight):
    pairs = pair_act.shape[0] * pair_act.shape[1]
    tiles = pltpu.VMEM((C, 8, 128), BF16)
    both = pltpu.VMEM((2, C, 8, 128), BF16)
    kept = pltpu.VMEM((GROUPS, C, 128), F32)
    flat = pltpu.VMEM((C * 8, 128), F32)
    out = pl.pallas_call(
        body,
        out_shape=jax.ShapeDtypeStruct((pairs, C), BF16),
        in_specs=[pl.BlockSpec(memory_space=pltpu.VMEM)] * 8,
        out_specs=pl.BlockSpec(memory_space=pltpu.VMEM),
        scratch_shapes=[
            pltpu.VMEM((5 * C, C), BF16),
            pltpu.VMEM((C, C), BF16),
            kept,
            pltpu.VMEM((GROUPS, 8, 128), F32),
            kept, kept, kept, kept, kept, kept, kept,
            flat, flat, flat,
            tiles, both, tiles, both, tiles, tiles, tiles, both,
            tiles, tiles, tiles, tiles,
            pltpu.VMEM((4, 16, 32, 128), F32),
            pltpu.VMEM((N, N), BF16),
            pltpu.VMEM((2, 2, 128, N), BF16),
            pltpu.VMEM((2, 2, 128, N), BF16),
            pltpu.VMEM((16, 32, 128), F32),
            pltpu.VMEM((4, 16, 16, 128), F32),
            pltpu.SemaphoreType.DMA((6,)),
            pltpu.SemaphoreType.DMA((6,)),
            pltpu.SemaphoreType.DMA((3,)),
            pltpu.SemaphoreType.DMA((3,)),
        ],
        compiler_params=pltpu.CompilerParams(
            collective_id=0, has_side_effects=True, vmem_limit_bytes=48 << 20
        ),
    )(
        pair_act.reshape(pairs, C),
        cotangent.reshape(pairs, C),
        in_gain.reshape(1, C),
        in_bias.reshape(1, C),
        proj_weight,
        out_gain.reshape(1, C),
        out_bias.reshape(1, C),
        out_weight,
    )
    return out.reshape(pair_act.shape)


def solution(mesh):
    placed = (P("row", "ch", None), P("row", "ch", None), P(), P(), P(), P(), P(), P())
    return jax.shard_map(
        on_device, mesh=mesh, in_specs=placed, out_specs=P("row", "ch", None), check_vma=False
    )
```

```python
import jax
import jax.numpy as jnp
from jax import lax
from jax.experimental import pallas as pl
from jax.experimental.pallas import tpu as pltpu
from jax.sharding import PartitionSpec as P

EPSILON = 1e-05
MESH = pl.DeviceIdType.MESH
F32 = jnp.float32
BF16 = jnp.bfloat16
C = 128
N = 512
GROUPS = 8
PLANES = 8
FAR = (2, 1, 3, 0)
RIGHT, LEFT, TRI, GRAD, GRAD_LEFT, GRAD_RIGHT = range(6)


def nn(a, b):
    return lax.dot_general(a, b, (((1,), (0,)), ((), ())), preferred_element_type=F32)


def swap_halves(a, b):
    axis = a.ndim - 1
    low = lax.broadcasted_iota(jnp.int32, a.shape, axis) < 64
    return (
        jnp.where(low, a, pltpu.roll(b, 64, axis)),
        jnp.where(low, pltpu.roll(a, 64, axis), b),
    )


def column(row_ref):
    return jnp.broadcast_to(row_ref[...], (C, C)).T


def distance(n):
    return 4 + ((n + 1) // 2) * (1 - 2 * lax.rem(n, 2))


def body(
    x_hbm, cot_hbm, ig_hbm, ib_hbm, w_hbm, og_hbm, ob_hbm, ow_hbm, out_ref,
    x_ref, cot_ref, ig_ref, ib_ref, w_ref, og_ref, ob_ref, ow_ref,
    wt, owt,
    normal, normed, sinv, left_a, left_b, right_a, right_b, gate, cot_t, grad_acc,
    hid, shift, stage,
    r_send, r_all, l_send, l_all, t_send, t_recv, g_send, g_all,
    gl_send, gl_recv, gr_send, gr_recv,
    r_f32, r_mat, r_matt, l_mat, gt_mat, gtt, gr_f32,
    in_sem, send_sem, recv_sem, core_send, core_recv,
):
    row = lax.axis_index("row")
    ch = lax.axis_index("ch")
    core = lax.rem(row, 2)
    other = 1 - core
    z = lax.rem(row // 2, 8)
    y = (row // 16) * 2 + ch // 4
    x = lax.rem(ch, 4)
    me = z * 16 + (row // 16) * 8 + ch
    partner = (row + 1 - 2 * core, ch)

    loads = [
        pltpu.make_async_copy(source, target, in_sem.at[i])
        for i, (source, target) in enumerate((
            (x_hbm, x_ref), (w_hbm, w_ref), (ig_hbm, ig_ref), (ib_hbm, ib_ref),
            (cot_hbm, cot_ref), (og_hbm, og_ref), (ob_hbm, ob_ref), (ow_hbm, ow_ref),
        ))
    ]
    for load in loads:
        load.start()

    ys = [lax.rem(y + d, 4) for d in FAR]
    xs = [lax.rem(x + d, 4) for d in FAR]
    chips = [(yy // 2, lax.rem(yy, 2) * 4 + xx) for yy in ys for xx in xs]

    def device(plane, chip):
        return ((chip[0] * 8 + plane) * 2 + core, chip[1])

    def slot(plane, chip):
        return plane * 16 + chip[0] * 8 + chip[1]

    def each_plane(step):
        lax.fori_loop(0, PLANES, lambda n, carry: (step(n), carry)[1], 0)

    barrier = pltpu.get_barrier_semaphore()
    pl.semaphore_signal(barrier, inc=1, device_id=partner, device_id_type=MESH)

    def greet(n):
        plane = lax.rem(z + distance(n), PLANES)
        for chip in chips[:-1]:
            pl.semaphore_signal(
                barrier, inc=1, device_id=device(plane, chip), device_id_type=MESH
            )

        @pl.when(n < PLANES - 1)
        def _():
            pl.semaphore_signal(
                barrier, inc=1, device_id=device(plane, chips[-1]), device_id_type=MESH
            )

    each_plane(greet)

    def send_plane(which, n, source, target):
        plane = lax.rem(z + distance(n), PLANES)

        def send(chip):
            pltpu.make_async_remote_copy(
                src_ref=source.at[slot(plane, chip)],
                dst_ref=target.at[me],
                send_sem=send_sem.at[which],
                recv_sem=recv_sem.at[which, z],
                device_id=device(plane, chip),
                device_id_type=MESH,
            ).start()

        for chip in chips[:-1]:
            send(chip)

        @pl.when(n < PLANES - 1)
        def _():
            send(chips[-1])

        @pl.when(n == PLANES - 1)
        def _():
            pltpu.make_async_copy(source.at[me], target.at[me], recv_sem.at[which, z]).start()

    def going_to(n):
        return lax.rem(z + distance(n), PLANES)

    def coming_from(n):
        return lax.rem(z + PLANES - distance(n), PLANES)

    def tiles(plane):
        return pl.ds(pl.multiple_of(plane * 16, 16), 16)

    def arrived(which, target, plane):
        part = target.at[tiles(plane)]
        pltpu.make_async_copy(part, part, recv_sem.at[which, plane]).wait()

    def sent(which, source):
        most = source.at[pl.ds(0, C - 1)]
        pltpu.make_async_copy(most, most, send_sem.at[which]).wait()

    def to_partner(which, buffer, plane):
        part = buffer.at[core, tiles(plane)]
        pltpu.make_async_remote_copy(
            src_ref=part,
            dst_ref=part,
            send_sem=core_send.at[which],
            recv_sem=core_recv.at[which, plane],
            device_id=partner,
            device_id_type=MESH,
        ).start()

    def from_partner(which, buffer, plane):
        part = buffer.at[other, tiles(plane)]
        pltpu.make_async_copy(part, part, core_recv.at[which, plane]).wait()

    def to_partner_sent(which, buffer):
        pltpu.make_async_copy(buffer.at[core], buffer.at[core], core_send.at[which]).wait()

    for load in loads[:4]:
        load.wait()
    wt[...] = w_ref[...].astype(F32).T.astype(BF16)
    in_gain = column(ig_ref)
    in_bias = column(ib_ref)
    for g in range(GROUPS):
        act = x_ref[pl.ds(g * 128, 128), :].astype(F32).T
        shifted = act - jnp.sum(act, axis=0, keepdims=True) * (1.0 / C)
        scale = lax.rsqrt(jnp.sum(shifted * shifted, axis=0, keepdims=True) * (1.0 / C) + EPSILON)
        hat = shifted * scale
        normed[g] = hat
        sinv[g] = jnp.broadcast_to(scale, (8, 128))
        normal[g] = (hat * in_gain + in_bias).astype(BF16)
        projected = nn(wt[pl.ds(256, 256), :], normal[g])
        val, sig = projected[:128], jax.nn.sigmoid(projected[128:])
        factor = sig * val
        right_a[g] = sig
        right_b[g] = factor * (1.0 - sig)
        stage[0, pl.ds(g, C, stride=8), :] = factor
    pl.semaphore_wait(barrier, C)

    def rows(plane):
        return pl.ds(pl.multiple_of(plane * 128, 128), 128)

    def send_factor(which, held, source, target):
        def step(n):
            plane = going_to(n)
            source[tiles(plane)] = stage[held, rows(plane), :].reshape(16, 8, 128).astype(BF16)
            send_plane(which, n, source, target)

        each_plane(step)

    send_factor(RIGHT, 0, r_send, r_all.at[core])

    for g in range(GROUPS):
        projected = nn(wt[pl.ds(0, 256), :], normal[g])
        val, sig = projected[:128], jax.nn.sigmoid(projected[128:])
        factor = sig * val
        left_a[g] = sig
        left_b[g] = factor * (1.0 - sig)
        stage[1, pl.ds(g, C, stride=8), :] = factor
    send_factor(LEFT, 1, l_send, l_all.at[core])

    for load in loads[4:]:
        load.wait()
    owt[...] = ow_ref[...].astype(F32).T.astype(BF16)
    out_gain = column(og_ref)
    mean_h = []
    for g in range(GROUPS):
        out_gate = jax.nn.sigmoid(nn(wt[pl.ds(512, 128), :], normal[g]))
        cotangent = cot_ref[pl.ds(g * 128, 128), :].astype(F32).T
        grad_mixed = cotangent * out_gate
        gate[g] = out_gate
        cot_t[g] = cotangent
        h = nn(ow_ref[...], grad_mixed.astype(BF16)) * out_gain
        hid[pl.ds(g, C, stride=8), :] = h
        mean_h.append(jnp.sum(h, axis=0, keepdims=True) * (1.0 / C))
    mean_h = jnp.concatenate(mean_h, axis=0)

    def place_right(half, plane):
        got = r_all[half, tiles(plane)].astype(F32).reshape(2, 8, 8, 128)
        for pair in range(4):
            even, odd = swap_halves(got[:, 2 * pair], got[:, 2 * pair + 1])
            for high in range(2):
                at = high * 8 + plane
                r_f32[pair, at, pl.ds(half * 16, 8, stride=2), :] = even[high]
                r_f32[pair, at, pl.ds(half * 16 + 1, 8, stride=2), :] = odd[high]

    def right_here(n):
        plane = coming_from(n)
        arrived(RIGHT, r_all.at[core], plane)
        to_partner(0, r_all, plane)
        place_right(core, plane)

    def right_there(n):
        plane = coming_from(n)
        from_partner(0, r_all, plane)
        place_right(other, plane)

    each_plane(right_here)
    each_plane(right_there)
    for pair in range(4):
        part = r_f32[pair].reshape(N, 128)
        r_mat[:, pl.ds(128 * pair, 128)] = part.astype(BF16)
        r_matt[pl.ds(128 * pair, 128), :] = part.T.astype(BF16)

    def place_pairs(buffer, half, plane, matrix):
        got = buffer[half, tiles(plane)].astype(F32).reshape(2, 8, 8, 128)
        parts = []
        for pair in range(4):
            even, odd = swap_halves(got[:, 2 * pair], got[:, 2 * pair + 1])
            parts.append(
                jnp.concatenate([even.reshape(16, 128), odd.reshape(16, 128)], axis=0).astype(BF16)
            )
        whole = jnp.concatenate(parts, axis=1)
        matrix[half, plane] = whole
        return whole

    def take_pieces(even, odd, buffer, plane):
        out = []
        for pair in range(4):
            out.extend(swap_halves(even(pair), odd(pair)))
        whole = jnp.stack(out, axis=1).reshape(16, 8, 128)
        buffer[tiles(plane)] = whole.astype(BF16)

    def take_rows(value, buffer, plane):
        def part(parity):
            return lambda pair: value[
                16 * parity : 16 * parity + 16, 128 * pair : 128 * pair + 128
            ].reshape(2, 8, 128)

        take_pieces(part(0), part(1), buffer, plane)

    def product(n):
        plane = coming_from(n)
        arrived(LEFT, l_all.at[core], plane)
        to_partner(1, l_all, plane)
        whole = place_pairs(l_all, core, plane, l_mat)
        take_rows(nn(whole, r_matt[...]), t_send, plane)

    def mirrored(n):
        return jnp.where(n == 0, 0, jnp.where(n == 7, 7, n + 2 * lax.rem(n, 2) - 1))

    def product_step(n):
        product(n)
        send_plane(TRI, mirrored(n), t_send, t_recv)

    each_plane(product_step)

    def left_there(n):
        plane = coming_from(n)
        from_partner(1, l_all, plane)
        place_pairs(l_all, other, plane, l_mat)

    each_plane(left_there)

    each_plane(lambda n: arrived(TRI, t_recv, coming_from(n)))
    tri = t_recv[...].astype(F32)
    mean_tri = jnp.sum(tri, axis=0) * (1.0 / C)
    shifted = tri - mean_tri[None]
    scale_tri = lax.rsqrt(jnp.sum(shifted * shifted, axis=0) * (1.0 / C) + EPSILON)
    shift[...] = shifted.reshape(C * 8, 128)
    second = jnp.sum(hid[...].reshape(C, 8, 128) * shifted, axis=0) * (scale_tri * (1.0 / C))
    weight = scale_tri * second

    def grad_step(n):
        plane = going_to(n)
        h = hid[rows(plane), :].reshape(16, 8, 128)
        off = shift[rows(plane), :].reshape(16, 8, 128)
        grad_tri = scale_tri[None] * (h - mean_h[None] - off * weight[None])
        g_send[tiles(plane)] = grad_tri.astype(BF16)
        send_plane(GRAD, n, g_send, g_all.at[core])

    each_plane(grad_step)

    out_bias = column(ob_ref)
    for g in range(GROUPS):
        hat = shift[pl.ds(g, C, stride=8), :] * scale_tri[g : g + 1]
        mixed = nn(owt[...], (hat * out_gain + out_bias).astype(BF16))
        out_gate = gate[g]
        grad_logit = cot_t[g] * mixed * out_gate * (1.0 - out_gate)
        grad_acc[g] = nn(w_ref[:, pl.ds(512, 128)], grad_logit.astype(BF16))

    def left_step(n):
        plane = coming_from(n)
        arrived(GRAD, g_all.at[core], plane)
        to_partner(2, g_all, plane)
        whole = place_pairs(g_all, core, plane, gt_mat)
        take_rows(nn(whole, r_mat[...]), gl_send, plane)
        send_plane(GRAD_LEFT, mirrored(n), gl_send, gl_recv)

    each_plane(left_step)

    def grad_there(n):
        plane = coming_from(n)
        from_partner(2, g_all, plane)
        place_pairs(g_all, other, plane, gt_mat)

    def grad_right(half):
        for pair in range(4):
            block = gt_mat[half, :, :, pl.ds(128 * pair, 128)].reshape(256, 128)
            gtt[pl.ds(4 * pair, 4)] = block.astype(F32).T.reshape(4, 32, 256)
        mine = gtt[:, pl.ds(pl.multiple_of(16 * core, 16), 16), :].reshape(256, 256)
        return nn(mine.astype(BF16), l_mat[half].reshape(256, N))

    total = grad_right(core)
    each_plane(grad_there)
    total = total + grad_right(other)
    for pair in range(4):
        gr_f32[pair] = total[:, 128 * pair : 128 * pair + 128].reshape(2, 8, 16, 128)

    def right_step(n):
        plane = going_to(n)

        def part(parity):
            return lambda pair: gr_f32[pair, :, plane, pl.ds(parity, 8, stride=2), :]

        take_pieces(part(0), part(1), gr_send, plane)
        send_plane(GRAD_RIGHT, n, gr_send, gr_recv)

    each_plane(right_step)

    def back(which, buffer, held):
        def step(n):
            plane = coming_from(n)
            arrived(which, buffer, plane)
            stage[held, rows(plane), :] = buffer[tiles(plane)].astype(F32).reshape(128, 128)

        each_plane(step)

    back(GRAD_LEFT, gl_recv, 0)
    for g in range(GROUPS):
        grad = stage[0, pl.ds(g, C, stride=8), :]
        both = jnp.concatenate([grad * left_a[g], grad * left_b[g]], axis=0).astype(BF16)
        grad_acc[g] += nn(w_ref[:, pl.ds(0, 256)], both)

    back(GRAD_RIGHT, gr_recv, 1)
    for g in range(GROUPS):
        grad = stage[1, pl.ds(g, C, stride=8), :]
        both = jnp.concatenate([grad * right_a[g], grad * right_b[g]], axis=0).astype(BF16)
        full = (grad_acc[g] + nn(w_ref[:, pl.ds(256, 256)], both)) * in_gain
        hat = normed[g]
        first = jnp.sum(full, axis=0, keepdims=True) * (1.0 / C)
        second = jnp.sum(full * hat, axis=0, keepdims=True) * (1.0 / C)
        grad_pair = sinv[g][:1] * (full - first - hat * second)
        out_ref[pl.ds(g * 128, 128), :] = grad_pair.T.astype(BF16)

    for which, source in enumerate((r_send, l_send, t_send, g_send, gl_send, gr_send)):
        sent(which, source)
    for which, buffer in enumerate((r_all, l_all, g_all)):
        to_partner_sent(which, buffer)


def on_device(pair_act, cotangent, in_gain, in_bias, proj_weight, out_gain, out_bias, out_weight):
    pairs = pair_act.shape[0] * pair_act.shape[1]
    operands = (
        pair_act.reshape(pairs, C),
        cotangent.reshape(pairs, C),
        in_gain.reshape(1, C),
        in_bias.reshape(1, C),
        proj_weight,
        out_gain.reshape(1, C),
        out_bias.reshape(1, C),
        out_weight,
    )
    pieces = pltpu.VMEM((C, 8, 128), BF16)
    both = pltpu.VMEM((2, C, 8, 128), BF16)
    kept = pltpu.VMEM((GROUPS, C, 128), F32)
    flat = pltpu.VMEM((C * 8, 128), F32)
    out = pl.pallas_call(
        body,
        out_shape=jax.ShapeDtypeStruct((pairs, C), BF16),
        in_specs=[pl.BlockSpec(memory_space=pl.ANY)] * 8,
        out_specs=pl.BlockSpec(memory_space=pltpu.VMEM),
        scratch_shapes=[pltpu.VMEM(a.shape, a.dtype) for a in operands] + [
            pltpu.VMEM((5 * C, C), BF16),
            pltpu.VMEM((C, C), BF16),
            pltpu.VMEM((GROUPS, C, 128), BF16),
            kept,
            pltpu.VMEM((GROUPS, 8, 128), F32),
            kept, kept, kept, kept, kept, kept, kept,
            flat, flat,
            pltpu.VMEM((2, C * 8, 128), F32),
            pieces, both, pieces, both, pieces, pieces, pieces, both,
            pieces, pieces, pieces, pieces,
            pltpu.VMEM((4, 16, 32, 128), F32),
            pltpu.VMEM((N, N), BF16),
            pltpu.VMEM((N, N), BF16),
            pltpu.VMEM((2, PLANES, 32, N), BF16),
            pltpu.VMEM((2, PLANES, 32, N), BF16),
            pltpu.VMEM((16, 32, 256), F32),
            pltpu.VMEM((4, 2, 8, 16, 128), F32),
            pltpu.SemaphoreType.DMA((8,)),
            pltpu.SemaphoreType.DMA((6,)),
            pltpu.SemaphoreType.DMA((6, PLANES)),
            pltpu.SemaphoreType.DMA((3,)),
            pltpu.SemaphoreType.DMA((3, PLANES)),
        ],
        compiler_params=pltpu.CompilerParams(
            collective_id=0, has_side_effects=True, vmem_limit_bytes=60 << 20
        ),
    )(*operands)
    return out.reshape(pair_act.shape)


def solution(mesh):
    placed = (P("row", "ch", None), P("row", "ch", None), P(), P(), P(), P(), P(), P())
    return jax.shard_map(
        on_device, mesh=mesh, in_specs=placed, out_specs=P("row", "ch", None), check_vma=False
    )
```

```python
import jax
import jax.numpy as jnp
from jax import lax
from jax.experimental import pallas as pl
from jax.experimental.pallas import tpu as pltpu
from jax.sharding import PartitionSpec as P

EPSILON = 1e-05
MESH = pl.DeviceIdType.MESH
F32 = jnp.float32
BF16 = jnp.bfloat16
C = 128
N = 512
GROUPS = 8
PLANES = 8
FAR = (2, 1, 3, 0)
FAR_PLANES = (4, 3, 5, 2, 6, 1, 7, 0)
RIGHT, LEFT, TRI, GRAD, GRAD_LEFT, GRAD_RIGHT = range(6)


def nn(a, b):
    return lax.dot_general(a, b, (((1,), (0,)), ((), ())), preferred_element_type=F32)


def swap_halves(a, b):
    axis = a.ndim - 1
    low = lax.broadcasted_iota(jnp.int32, a.shape, axis) < 64
    return (
        jnp.where(low, a, pltpu.roll(b, 64, axis)),
        jnp.where(low, pltpu.roll(a, 64, axis), b),
    )


def column(row_ref):
    return jnp.broadcast_to(row_ref[...], (C, C)).T


def distance(n):
    return jnp.where(n == 0, 0, 4 + (n // 2) * (2 * lax.rem(n, 2) - 1))


def body(
    x_hbm, cot_hbm, ig_hbm, ib_hbm, w_hbm, og_hbm, ob_hbm, ow_hbm, out_ref,
    x_ref, cot_ref, ig_ref, ib_ref, w_ref, og_ref, ob_ref, ow_ref,
    wt, owt,
    normal, normed, sinv, left_a, left_b, right_a, right_b, gate, cot_t, grad_acc,
    hid, shift, stage,
    r_send, r_all, l_send, l_all, t_send, t_recv, g_send, g_all,
    gl_send, gl_recv, gr_send, gr_recv,
    r_f32, r_mat, r_matt, l_mat, gt_mat, gtt, gr_f32,
    in_sem, send_sem, recv_sem, core_send, core_recv,
):
    row = lax.axis_index("row")
    ch = lax.axis_index("ch")
    core = lax.rem(row, 2)
    other = 1 - core
    z = lax.rem(row // 2, 8)
    y = (row // 16) * 2 + ch // 4
    x = lax.rem(ch, 4)
    me = z * 16 + (row // 16) * 8 + ch
    partner = (row + 1 - 2 * core, ch)

    loads = [
        pltpu.make_async_copy(source, target, in_sem.at[i])
        for i, (source, target) in enumerate((
            (x_hbm, x_ref), (w_hbm, w_ref), (ig_hbm, ig_ref), (ib_hbm, ib_ref),
            (cot_hbm, cot_ref), (og_hbm, og_ref), (ob_hbm, ob_ref), (ow_hbm, ow_ref),
        ))
    ]
    for load in loads:
        load.start()

    ys = [lax.rem(y + d, 4) for d in FAR]
    xs = [lax.rem(x + d, 4) for d in FAR]
    chips = [(yy // 2, lax.rem(yy, 2) * 4 + xx) for yy in ys for xx in xs]

    def device(plane, chip):
        return ((chip[0] * 8 + plane) * 2 + core, chip[1])

    def slot(plane, chip):
        return plane * 16 + chip[0] * 8 + chip[1]

    def each_plane(step):
        lax.fori_loop(0, PLANES, lambda n, carry: (step(n), carry)[1], 0)

    barrier = pltpu.get_barrier_semaphore()
    pl.semaphore_signal(barrier, inc=1, device_id=partner, device_id_type=MESH)

    def greet(n):
        plane = lax.rem(z + distance(n), PLANES)
        for chip in chips[:-1]:
            pl.semaphore_signal(
                barrier, inc=1, device_id=device(plane, chip), device_id_type=MESH
            )

        @pl.when(n > 0)
        def _():
            pl.semaphore_signal(
                barrier, inc=1, device_id=device(plane, chips[-1]), device_id_type=MESH
            )

    each_plane(greet)

    def send_plane(which, n, source, target):
        plane = lax.rem(z + distance(n), PLANES)

        def send(chip):
            pltpu.make_async_remote_copy(
                src_ref=source.at[slot(plane, chip)],
                dst_ref=target.at[me],
                send_sem=send_sem.at[which],
                recv_sem=recv_sem.at[which, z],
                device_id=device(plane, chip),
                device_id_type=MESH,
            ).start()

        for chip in chips[:-1]:
            send(chip)

        @pl.when(n > 0)
        def _():
            send(chips[-1])

        @pl.when(n == 0)
        def _():
            pltpu.make_async_copy(source.at[me], target.at[me], recv_sem.at[which, z]).start()

    zs = [lax.rem(z + d, PLANES) for d in FAR_PLANES]

    def row_base(step):
        yy = lax.rem(y + 2 + ((step + 1) // 2) * (1 - 2 * lax.rem(step, 2)), 4)
        return yy // 2, lax.rem(yy, 2) * 4

    def send_row(which, step, source, target):
        high, low = row_base(step)
        for dx, xx in zip(FAR, xs):
            for dz, plane in zip(FAR_PLANES, zs):
                chip = (high, low + xx)

                def send():
                    pltpu.make_async_remote_copy(
                        src_ref=source.at[slot(plane, chip)],
                        dst_ref=target.at[me],
                        send_sem=send_sem.at[which],
                        recv_sem=recv_sem.at[which, z],
                        device_id=device(plane, chip),
                        device_id_type=MESH,
                    ).start()

                if dx or dz:
                    send()
                else:
                    pl.when(step < 3)(send)

                    @pl.when(step == 3)
                    def _():
                        own = pltpu.make_async_copy(
                            source.at[me], target.at[me], recv_sem.at[which, z]
                        )
                        own.start()

    def each_row(step):
        lax.fori_loop(0, 4, lambda n, carry: (step(n), carry)[1], 0)

    def going_to(n):
        return lax.rem(z + distance(n), PLANES)

    def coming_from(n):
        return lax.rem(z + PLANES - distance(n), PLANES)

    def tiles(plane):
        return pl.ds(pl.multiple_of(plane * 16, 16), 16)

    def arrived(which, target, plane):
        part = target.at[tiles(plane)]
        pltpu.make_async_copy(part, part, recv_sem.at[which, plane]).wait()

    def sent(which, source):
        most = source.at[pl.ds(0, C - 1)]
        pltpu.make_async_copy(most, most, send_sem.at[which]).wait()

    def to_partner(which, buffer, plane):
        part = buffer.at[core, tiles(plane)]
        pltpu.make_async_remote_copy(
            src_ref=part,
            dst_ref=part,
            send_sem=core_send.at[which],
            recv_sem=core_recv.at[which, plane],
            device_id=partner,
            device_id_type=MESH,
        ).start()

    def from_partner(which, buffer, plane):
        part = buffer.at[other, tiles(plane)]
        pltpu.make_async_copy(part, part, core_recv.at[which, plane]).wait()

    def to_partner_sent(which, buffer):
        pltpu.make_async_copy(buffer.at[core], buffer.at[core], core_send.at[which]).wait()

    for load in loads[:4]:
        load.wait()
    wt[...] = w_ref[...].astype(F32).T.astype(BF16)
    in_gain = column(ig_ref)
    in_bias = column(ib_ref)
    for g in range(GROUPS):
        act = x_ref[pl.ds(g * 128, 128), :].astype(F32).T
        shifted = act - jnp.sum(act, axis=0, keepdims=True) * (1.0 / C)
        scale = lax.rsqrt(jnp.sum(shifted * shifted, axis=0, keepdims=True) * (1.0 / C) + EPSILON)
        hat = shifted * scale
        normed[g] = hat
        sinv[g] = jnp.broadcast_to(scale, (8, 128))
        normal[g] = (hat * in_gain + in_bias).astype(BF16)
        projected = nn(wt[pl.ds(256, 256), :], normal[g])
        val, sig = projected[:128], jax.nn.sigmoid(projected[128:])
        factor = sig * val
        right_a[g] = sig
        right_b[g] = factor * (1.0 - sig)
        stage[0, pl.ds(g, C, stride=8), :] = factor
    pl.semaphore_wait(barrier, C)

    def rows(plane):
        return pl.ds(pl.multiple_of(plane * 128, 128), 128)

    def send_left(n):
        plane = going_to(n)
        l_send[tiles(plane)] = stage[1, rows(plane), :].reshape(16, 8, 128).astype(BF16)
        send_plane(LEFT, n, l_send, l_all.at[core])

    def row_tiles(plane, base):
        return pl.ds(pl.multiple_of(plane * 16 + base, 4), 4)

    def row_rows(plane, base):
        return pl.ds(pl.multiple_of((plane * 16 + base) * 8, 32), 32)

    def send_right(n):
        plane = going_to(n)
        r_send[tiles(plane)] = stage[0, rows(plane), :].reshape(16, 8, 128).astype(BF16)
        send_plane(RIGHT, n, r_send, r_all.at[core])

    each_plane(send_right)

    for g in range(GROUPS):
        projected = nn(wt[pl.ds(0, 256), :], normal[g])
        val, sig = projected[:128], jax.nn.sigmoid(projected[128:])
        factor = sig * val
        left_a[g] = sig
        left_b[g] = factor * (1.0 - sig)
        stage[1, pl.ds(g, C, stride=8), :] = factor
    each_plane(send_left)

    for load in loads[4:]:
        load.wait()
    owt[...] = ow_ref[...].astype(F32).T.astype(BF16)
    out_gain = column(og_ref)
    mean_h = []
    for g in range(GROUPS):
        out_gate = jax.nn.sigmoid(nn(wt[pl.ds(512, 128), :], normal[g]))
        cotangent = cot_ref[pl.ds(g * 128, 128), :].astype(F32).T
        grad_mixed = cotangent * out_gate
        gate[g] = out_gate
        cot_t[g] = cotangent
        h = nn(ow_ref[...], grad_mixed.astype(BF16)) * out_gain
        hid[pl.ds(g, C, stride=8), :] = h
        mean_h.append(jnp.sum(h, axis=0, keepdims=True) * (1.0 / C))
    mean_h = jnp.concatenate(mean_h, axis=0)

    def place_right(half, plane):
        got = r_all[half, tiles(plane)].astype(F32).reshape(2, 8, 8, 128)
        for pair in range(4):
            even, odd = swap_halves(got[:, 2 * pair], got[:, 2 * pair + 1])
            for high in range(2):
                at = high * 8 + plane
                r_f32[pair, at, pl.ds(half * 16, 8, stride=2), :] = even[high]
                r_f32[pair, at, pl.ds(half * 16 + 1, 8, stride=2), :] = odd[high]

    def right_here(n):
        plane = coming_from(n)
        arrived(RIGHT, r_all.at[core], plane)
        to_partner(0, r_all, plane)
        place_right(core, plane)

    each_plane(right_here)
    each_plane(lambda n: from_partner(0, r_all, coming_from(n)))
    for pair in range(4):
        got = r_all[other].reshape(PLANES, 2, 8, 8, 128)
        even, odd = swap_halves(
            got[:, :, 2 * pair].astype(F32).reshape(16, 8, 128),
            got[:, :, 2 * pair + 1].astype(F32).reshape(16, 8, 128),
        )
        for at in range(16):
            to = (at % 2) * 8 + at // 2
            r_f32[pair, to, pl.ds(other * 16, 8, stride=2), :] = even[at]
            r_f32[pair, to, pl.ds(other * 16 + 1, 8, stride=2), :] = odd[at]
    for pair in range(4):
        part = r_f32[pair].reshape(N, 128)
        r_mat[:, pl.ds(128 * pair, 128)] = part.astype(BF16)
        r_matt[pl.ds(128 * pair, 128), :] = part.T.astype(BF16)

    def place_pairs(buffer, half, plane, matrix):
        got = buffer[half, tiles(plane)].astype(F32).reshape(2, 8, 8, 128)
        parts = []
        for pair in range(4):
            even, odd = swap_halves(got[:, 2 * pair], got[:, 2 * pair + 1])
            parts.append(
                jnp.concatenate([even.reshape(16, 128), odd.reshape(16, 128)], axis=0).astype(BF16)
            )
        whole = jnp.concatenate(parts, axis=1)
        matrix[half, plane] = whole
        return whole

    def take_pieces(even, odd, buffer, plane):
        out = []
        for pair in range(4):
            out.extend(swap_halves(even(pair), odd(pair)))
        whole = jnp.stack(out, axis=1).reshape(16, 8, 128)
        buffer[tiles(plane)] = whole.astype(BF16)

    def take_rows(value, buffer, plane):
        def part(parity):
            return lambda pair: value[
                16 * parity : 16 * parity + 16, 128 * pair : 128 * pair + 128
            ].reshape(2, 8, 128)

        take_pieces(part(0), part(1), buffer, plane)

    def mirrored(n):
        return jnp.where(n < 2, n, n + 1 - 2 * lax.rem(n, 2))

    def multiply(got, link, buffer, matrix, factor, replied, send, target):
        def step(pair, carry):
            steps = (2 * pair, 2 * pair + 1)
            planes = [coming_from(n) for n in steps]
            wholes = []
            for plane in planes:
                arrived(got, buffer.at[core], plane)
                to_partner(link, buffer, plane)
                wholes.append(place_pairs(buffer, core, plane, matrix))
            value = nn(jnp.concatenate(wholes, axis=0), factor[...])
            for i, plane in enumerate(planes):
                take_rows(value[32 * i : 32 * i + 32], send, plane)
                send_plane(replied, mirrored(steps[i]), send, target)
            return carry

        lax.fori_loop(0, PLANES // 2, step, 0)

    def fetch(link, buffer, matrix):
        each_plane(lambda n: from_partner(link, buffer, coming_from(n)))
        got = buffer[other].reshape(PLANES, 2, 8, 8, 128)
        for pair in range(4):
            even, odd = swap_halves(
                got[:, :, 2 * pair].astype(F32), got[:, :, 2 * pair + 1].astype(F32)
            )
            part = jnp.stack([even, odd], axis=1).reshape(PLANES, 32, 128)
            matrix[other, :, :, pl.ds(128 * pair, 128)] = part.astype(BF16)

    multiply(LEFT, 1, l_all, l_mat, r_matt, TRI, t_send, t_recv)
    fetch(1, l_all, l_mat)

    each_plane(lambda n: arrived(TRI, t_recv, coming_from(n)))
    tri = t_recv[...].astype(F32)
    mean_tri = jnp.sum(tri, axis=0) * (1.0 / C)
    shifted = tri - mean_tri[None]
    scale_tri = lax.rsqrt(jnp.sum(shifted * shifted, axis=0) * (1.0 / C) + EPSILON)
    shift[...] = shifted.reshape(C * 8, 128)
    second = jnp.sum(hid[...].reshape(C, 8, 128) * shifted, axis=0) * (scale_tri * (1.0 / C))
    weight = scale_tri * second

    def grad_step(n):
        plane = going_to(n)
        h = hid[rows(plane), :].reshape(16, 8, 128)
        off = shift[rows(plane), :].reshape(16, 8, 128)
        grad_tri = scale_tri[None] * (h - mean_h[None] - off * weight[None])
        g_send[tiles(plane)] = grad_tri.astype(BF16)
        send_plane(GRAD, n, g_send, g_all.at[core])

    each_plane(grad_step)

    out_bias = column(ob_ref)
    for g in range(GROUPS):
        hat = shift[pl.ds(g, C, stride=8), :] * scale_tri[g : g + 1]
        mixed = nn(owt[...], (hat * out_gain + out_bias).astype(BF16))
        out_gate = gate[g]
        grad_logit = cot_t[g] * mixed * out_gate * (1.0 - out_gate)
        grad_acc[g] = nn(w_ref[:, pl.ds(512, 128)], grad_logit.astype(BF16))

    multiply(GRAD, 2, g_all, gt_mat, r_mat, GRAD_LEFT, gl_send, gl_recv)
    fetch(2, g_all, gt_mat)
    for pair in range(4):
        block = gt_mat[:, :, :, pl.ds(128 * pair, 128)].reshape(N, 128)
        gtt[pl.ds(4 * pair, 4)] = block.astype(F32).T.reshape(4, 32, N)
    mine = gtt[:, pl.ds(pl.multiple_of(16 * core, 16), 16), :].reshape(256, N)
    total = nn(mine.astype(BF16), l_mat[...].reshape(N, N))
    for pair in range(4):
        gr_f32[pair] = total[:, 128 * pair : 128 * pair + 128].reshape(2, 8, 16, 128)

    def right_step(step):
        high, low = row_base(step)
        for k in range(2):
            pair = low // 2 + k
            both = swap_halves(
                gr_f32[pair, high, :, pl.ds(0, 8, stride=2), :],
                gr_f32[pair, high, :, pl.ds(1, 8, stride=2), :],
            )
            for e in range(2):
                piece = both[e].astype(BF16)
                for plane in range(PLANES):
                    gr_send[plane * 16 + high * 8 + low + 2 * k + e] = piece[plane]
        send_row(GRAD_RIGHT, step, gr_send, gr_recv)

    each_row(right_step)

    def back(which, buffer, held):
        def step(n):
            plane = coming_from(n)
            arrived(which, buffer, plane)
            stage[held, rows(plane), :] = buffer[tiles(plane)].astype(F32).reshape(128, 128)

        each_plane(step)

    back(GRAD_LEFT, gl_recv, 0)
    for g in range(GROUPS):
        grad = stage[0, pl.ds(g, C, stride=8), :]
        both = jnp.concatenate([grad * left_a[g], grad * left_b[g]], axis=0).astype(BF16)
        grad_acc[g] += nn(w_ref[:, pl.ds(0, 256)], both)

    back(GRAD_RIGHT, gr_recv, 1)
    for g in range(GROUPS):
        grad = stage[1, pl.ds(g, C, stride=8), :]
        both = jnp.concatenate([grad * right_a[g], grad * right_b[g]], axis=0).astype(BF16)
        full = (grad_acc[g] + nn(w_ref[:, pl.ds(256, 256)], both)) * in_gain
        hat = normed[g]
        first = jnp.sum(full, axis=0, keepdims=True) * (1.0 / C)
        second = jnp.sum(full * hat, axis=0, keepdims=True) * (1.0 / C)
        grad_pair = sinv[g][:1] * (full - first - hat * second)
        out_ref[pl.ds(g * 128, 128), :] = grad_pair.T.astype(BF16)

    for which, source in enumerate((r_send, l_send, t_send, g_send, gl_send, gr_send)):
        sent(which, source)
    for which, buffer in enumerate((r_all, l_all, g_all)):
        to_partner_sent(which, buffer)


def on_device(pair_act, cotangent, in_gain, in_bias, proj_weight, out_gain, out_bias, out_weight):
    pairs = pair_act.shape[0] * pair_act.shape[1]
    operands = (
        pair_act.reshape(pairs, C),
        cotangent.reshape(pairs, C),
        in_gain.reshape(1, C),
        in_bias.reshape(1, C),
        proj_weight,
        out_gain.reshape(1, C),
        out_bias.reshape(1, C),
        out_weight,
    )
    pieces = pltpu.VMEM((C, 8, 128), BF16)
    both = pltpu.VMEM((2, C, 8, 128), BF16)
    kept = pltpu.VMEM((GROUPS, C, 128), F32)
    flat = pltpu.VMEM((C * 8, 128), F32)
    out = pl.pallas_call(
        body,
        out_shape=pltpu.VMEM((pairs, C), BF16),
        in_specs=[pl.BlockSpec(memory_space=pl.ANY)] * 8,
        out_specs=pl.BlockSpec(memory_space=pltpu.VMEM),
        scratch_shapes=[pltpu.VMEM(a.shape, a.dtype) for a in operands] + [
            pltpu.VMEM((5 * C, C), BF16),
            pltpu.VMEM((C, C), BF16),
            pltpu.VMEM((GROUPS, C, 128), BF16),
            kept,
            pltpu.VMEM((GROUPS, 8, 128), F32),
            kept, kept, kept, kept, kept, kept, kept,
            flat, flat,
            pltpu.VMEM((2, C * 8, 128), F32),
            pieces, both, pieces, both, pieces, pieces, pieces, both,
            pieces, pieces, pieces, pieces,
            pltpu.VMEM((4, 16, 32, 128), F32),
            pltpu.VMEM((N, N), BF16),
            pltpu.VMEM((N, N), BF16),
            pltpu.VMEM((2, PLANES, 32, N), BF16),
            pltpu.VMEM((2, PLANES, 32, N), BF16),
            pltpu.VMEM((16, 32, N), F32),
            pltpu.VMEM((4, 2, 8, 16, 128), F32),
            pltpu.SemaphoreType.DMA((8,)),
            pltpu.SemaphoreType.DMA((6,)),
            pltpu.SemaphoreType.DMA((6, PLANES)),
            pltpu.SemaphoreType.DMA((3,)),
            pltpu.SemaphoreType.DMA((3, PLANES)),
        ],
        compiler_params=pltpu.CompilerParams(
            collective_id=0, has_side_effects=True, vmem_limit_bytes=56 << 20
        ),
    )(*operands)
    return out.reshape(pair_act.shape)


def solution(mesh):
    placed = (P("row", "ch", None), P("row", "ch", None), P(), P(), P(), P(), P(), P())
    return jax.shard_map(
        on_device, mesh=mesh, in_specs=placed, out_specs=P("row", "ch", None), check_vma=False
    )
```

```python
import jax
import jax.numpy as jnp
from jax import lax
from jax.experimental import pallas as pl
from jax.experimental.pallas import tpu as pltpu
from jax.sharding import PartitionSpec as P

EPSILON = 1e-05
MESH = pl.DeviceIdType.MESH
F32 = jnp.float32
BF16 = jnp.bfloat16
C = 128
N = 512
GROUPS = 8
PLANES = 8
FAR = (2, 1, 3, 0)
FAR_PLANES = (4, 3, 5, 2, 6, 1, 7, 0)
RIGHT, LEFT, TRI, GRAD, GRAD_LEFT, GRAD_RIGHT = range(6)


def nn(a, b):
    return lax.dot_general(a, b, (((1,), (0,)), ((), ())), preferred_element_type=F32)


def swap_halves(a, b):
    axis = a.ndim - 1
    low = lax.broadcasted_iota(jnp.int32, a.shape, axis) < 64
    return (
        jnp.where(low, a, pltpu.roll(b, 64, axis)),
        jnp.where(low, pltpu.roll(a, 64, axis), b),
    )


def column(row_ref):
    return jnp.broadcast_to(row_ref[...], (C, C)).T


def distance(n):
    return jnp.where(n == 0, 0, 4 + (n // 2) * (2 * lax.rem(n, 2) - 1))


def body(
    x_hbm, cot_hbm, ig_hbm, ib_hbm, w_hbm, og_hbm, ob_hbm, ow_hbm, out_ref,
    x_ref, cot_ref, ig_ref, ib_ref, w_ref, og_ref, ob_ref, ow_ref,
    wt, owt,
    normal, normed, sinv, left_a, left_b, right_a, right_b, gate, cot_t, grad_acc,
    hid, shift, stage,
    r_send, r_all, l_send, l_all, t_send, t_recv, g_send, g_all,
    gl_send, gl_recv, gr_send, gr_recv,
    r_f32, r_mat, r_matt, l_mat, gt_mat, gtt, gr_f32,
    in_sem, send_sem, recv_sem, core_send, core_recv,
):
    row = lax.axis_index("row")
    ch = lax.axis_index("ch")
    core = lax.rem(row, 2)
    other = 1 - core
    z = lax.rem(row // 2, 8)
    y = (row // 16) * 2 + ch // 4
    x = lax.rem(ch, 4)
    me = z * 16 + (row // 16) * 8 + ch
    partner = (row + 1 - 2 * core, ch)

    loads = [
        pltpu.make_async_copy(source, target, in_sem.at[i])
        for i, (source, target) in enumerate((
            (x_hbm, x_ref), (w_hbm, w_ref), (ig_hbm, ig_ref), (ib_hbm, ib_ref),
            (cot_hbm, cot_ref), (og_hbm, og_ref), (ob_hbm, ob_ref), (ow_hbm, ow_ref),
        ))
    ]
    for load in loads:
        load.start()

    ys = [lax.rem(y + d, 4) for d in FAR]
    xs = [lax.rem(x + d, 4) for d in FAR]
    chips = [(yy // 2, lax.rem(yy, 2) * 4 + xx) for yy in ys for xx in xs]

    def device(plane, chip):
        return ((chip[0] * 8 + plane) * 2 + core, chip[1])

    def slot(plane, chip):
        return plane * 16 + chip[0] * 8 + chip[1]

    def each_plane(step):
        lax.fori_loop(0, PLANES, lambda n, carry: (step(n), carry)[1], 0)

    barrier = pltpu.get_barrier_semaphore()
    pl.semaphore_signal(barrier, inc=1, device_id=partner, device_id_type=MESH)

    def greet(n):
        plane = lax.rem(z + distance(n), PLANES)
        for chip in chips[:-1]:
            pl.semaphore_signal(
                barrier, inc=1, device_id=device(plane, chip), device_id_type=MESH
            )

        @pl.when(n > 0)
        def _():
            pl.semaphore_signal(
                barrier, inc=1, device_id=device(plane, chips[-1]), device_id_type=MESH
            )

    each_plane(greet)

    def send_plane(which, n, source, target):
        plane = lax.rem(z + distance(n), PLANES)

        def send(chip):
            pltpu.make_async_remote_copy(
                src_ref=source.at[slot(plane, chip)],
                dst_ref=target.at[me],
                send_sem=send_sem.at[which],
                recv_sem=recv_sem.at[which, z],
                device_id=device(plane, chip),
                device_id_type=MESH,
            ).start()

        for chip in chips[:-1]:
            send(chip)

        @pl.when(n > 0)
        def _():
            send(chips[-1])

        @pl.when(n == 0)
        def _():
            pltpu.make_async_copy(source.at[me], target.at[me], recv_sem.at[which, z]).start()

    zs = [lax.rem(z + d, PLANES) for d in FAR_PLANES]

    def row_base(step):
        yy = lax.rem(y + 2 + ((step + 1) // 2) * (1 - 2 * lax.rem(step, 2)), 4)
        return yy // 2, lax.rem(yy, 2) * 4

    def send_row(which, step, source, target):
        high, low = row_base(step)
        for dx, xx in zip(FAR, xs):
            for dz, plane in zip(FAR_PLANES, zs):
                chip = (high, low + xx)

                def send():
                    pltpu.make_async_remote_copy(
                        src_ref=source.at[slot(plane, chip)],
                        dst_ref=target.at[me],
                        send_sem=send_sem.at[which],
                        recv_sem=recv_sem.at[which, z],
                        device_id=device(plane, chip),
                        device_id_type=MESH,
                    ).start()

                if dx or dz:
                    send()
                else:
                    pl.when(step < 3)(send)

                    @pl.when(step == 3)
                    def _():
                        own = pltpu.make_async_copy(
                            source.at[me], target.at[me], recv_sem.at[which, z]
                        )
                        own.start()

    def each_row(step):
        lax.fori_loop(0, 4, lambda n, carry: (step(n), carry)[1], 0)

    def going_to(n):
        return lax.rem(z + distance(n), PLANES)

    def coming_from(n):
        return lax.rem(z + PLANES - distance(n), PLANES)

    def tiles(plane):
        return pl.ds(pl.multiple_of(plane * 16, 16), 16)

    def arrived(which, target, plane):
        part = target.at[tiles(plane)]
        pltpu.make_async_copy(part, part, recv_sem.at[which, plane]).wait()

    def sent(which, source):
        most = source.at[pl.ds(0, C - 1)]
        pltpu.make_async_copy(most, most, send_sem.at[which]).wait()

    def to_partner(which, buffer, plane):
        part = buffer.at[core, tiles(plane)]
        pltpu.make_async_remote_copy(
            src_ref=part,
            dst_ref=part,
            send_sem=core_send.at[which],
            recv_sem=core_recv.at[which, plane],
            device_id=partner,
            device_id_type=MESH,
        ).start()

    def from_partner(which, buffer, plane):
        part = buffer.at[other, tiles(plane)]
        pltpu.make_async_copy(part, part, core_recv.at[which, plane]).wait()

    def to_partner_sent(which, buffer):
        pltpu.make_async_copy(buffer.at[core], buffer.at[core], core_send.at[which]).wait()

    for load in loads[:4]:
        load.wait()
    wt[...] = w_ref[...].astype(F32).T.astype(BF16)
    in_gain = column(ig_ref)
    in_bias = column(ib_ref)
    for g in range(GROUPS):
        act = x_ref[pl.ds(g * 128, 128), :].astype(F32).T
        shifted = act - jnp.sum(act, axis=0, keepdims=True) * (1.0 / C)
        scale = lax.rsqrt(jnp.sum(shifted * shifted, axis=0, keepdims=True) * (1.0 / C) + EPSILON)
        hat = shifted * scale
        normed[g] = hat
        sinv[g] = jnp.broadcast_to(scale, (8, 128))
        normal[g] = (hat * in_gain + in_bias).astype(BF16)
        projected = nn(wt[pl.ds(256, 256), :], normal[g])
        val, sig = projected[:128], jax.nn.sigmoid(projected[128:])
        factor = sig * val
        right_a[g] = sig
        right_b[g] = factor * (1.0 - sig)
        stage[0, pl.ds(g, C, stride=8), :] = factor
    pl.semaphore_wait(barrier, C)

    def rows(plane):
        return pl.ds(pl.multiple_of(plane * 128, 128), 128)

    def send_left(n):
        plane = going_to(n)
        l_send[tiles(plane)] = stage[1, rows(plane), :].reshape(16, 8, 128).astype(BF16)
        send_plane(LEFT, n, l_send, l_all.at[core])

    def row_tiles(plane, base):
        return pl.ds(pl.multiple_of(plane * 16 + base, 4), 4)

    def row_rows(plane, base):
        return pl.ds(pl.multiple_of((plane * 16 + base) * 8, 32), 32)

    def send_right(n):
        plane = going_to(n)
        r_send[tiles(plane)] = stage[0, rows(plane), :].reshape(16, 8, 128).astype(BF16)
        send_plane(RIGHT, n, r_send, r_all.at[core])

    each_plane(send_right)

    for g in range(GROUPS):
        projected = nn(wt[pl.ds(0, 256), :], normal[g])
        val, sig = projected[:128], jax.nn.sigmoid(projected[128:])
        factor = sig * val
        left_a[g] = sig
        left_b[g] = factor * (1.0 - sig)
        stage[1, pl.ds(g, C, stride=8), :] = factor
    each_plane(send_left)

    for load in loads[4:]:
        load.wait()
    owt[...] = ow_ref[...].astype(F32).T.astype(BF16)
    out_gain = column(og_ref)
    mean_h = []
    for g in range(GROUPS):
        out_gate = jax.nn.sigmoid(nn(wt[pl.ds(512, 128), :], normal[g]))
        cotangent = cot_ref[pl.ds(g * 128, 128), :].astype(F32).T
        grad_mixed = cotangent * out_gate
        gate[g] = out_gate
        cot_t[g] = cotangent
        h = nn(ow_ref[...], grad_mixed.astype(BF16)) * out_gain
        hid[pl.ds(g, C, stride=8), :] = h
        mean_h.append(jnp.sum(h, axis=0, keepdims=True) * (1.0 / C))
    mean_h = jnp.concatenate(mean_h, axis=0)

    def place_right(half, plane):
        got = r_all[half, tiles(plane)].astype(F32).reshape(2, 8, 8, 128)
        for pair in range(4):
            even, odd = swap_halves(got[:, 2 * pair], got[:, 2 * pair + 1])
            for high in range(2):
                at = high * 8 + plane
                r_f32[pair, at, pl.ds(half * 16, 8, stride=2), :] = even[high]
                r_f32[pair, at, pl.ds(half * 16 + 1, 8, stride=2), :] = odd[high]

    def right_here(n):
        plane = coming_from(n)
        arrived(RIGHT, r_all.at[core], plane)
        to_partner(0, r_all, plane)
        place_right(core, plane)

    each_plane(right_here)
    each_plane(lambda n: from_partner(0, r_all, coming_from(n)))
    for pair in range(4):
        got = r_all[other].reshape(PLANES, 2, 8, 8, 128)
        even, odd = swap_halves(
            got[:, :, 2 * pair].astype(F32).reshape(16, 8, 128),
            got[:, :, 2 * pair + 1].astype(F32).reshape(16, 8, 128),
        )
        for at in range(16):
            to = (at % 2) * 8 + at // 2
            r_f32[pair, to, pl.ds(other * 16, 8, stride=2), :] = even[at]
            r_f32[pair, to, pl.ds(other * 16 + 1, 8, stride=2), :] = odd[at]
    for pair in range(4):
        part = r_f32[pair].reshape(N, 128)
        r_mat[:, pl.ds(128 * pair, 128)] = part.astype(BF16)
        r_matt[pl.ds(128 * pair, 128), :] = part.T.astype(BF16)

    def place_pairs(buffer, half, plane, matrix):
        got = buffer[half, tiles(plane)].astype(F32).reshape(2, 8, 8, 128)
        parts = []
        for pair in range(4):
            even, odd = swap_halves(got[:, 2 * pair], got[:, 2 * pair + 1])
            parts.append(
                jnp.concatenate([even.reshape(16, 128), odd.reshape(16, 128)], axis=0).astype(BF16)
            )
        whole = jnp.concatenate(parts, axis=1)
        matrix[half, plane] = whole
        return whole

    def take_pieces(even, odd, buffer, plane):
        out = []
        for pair in range(4):
            out.extend(swap_halves(even(pair), odd(pair)))
        whole = jnp.stack(out, axis=1).reshape(16, 8, 128)
        buffer[tiles(plane)] = whole.astype(BF16)

    def take_rows(value, buffer, plane):
        def part(parity):
            return lambda pair: value[
                16 * parity : 16 * parity + 16, 128 * pair : 128 * pair + 128
            ].reshape(2, 8, 128)

        take_pieces(part(0), part(1), buffer, plane)

    def mirrored(n):
        return jnp.where(n < 2, n, n + 1 - 2 * lax.rem(n, 2))

    def multiply(got, link, buffer, matrix, factor, replied, send, target):
        def step(steps):
            planes = [coming_from(n) for n in steps]
            wholes = []
            for plane in planes:
                arrived(got, buffer.at[core], plane)
                to_partner(link, buffer, plane)
                wholes.append(place_pairs(buffer, core, plane, matrix))
            value = nn(jnp.concatenate(wholes, axis=0), factor[...])
            for i, plane in enumerate(planes):
                take_rows(value[32 * i : 32 * i + 32], send, plane)
                send_plane(replied, mirrored(steps[i]), send, target)

        for steps in ((1,), (2, 3), (0, 4, 5), (6, 7)):
            step(steps)

    def fetch(link, buffer, matrix):
        each_plane(lambda n: from_partner(link, buffer, coming_from(n)))
        got = buffer[other].reshape(PLANES, 2, 8, 8, 128)
        for pair in range(4):
            even, odd = swap_halves(
                got[:, :, 2 * pair].astype(F32), got[:, :, 2 * pair + 1].astype(F32)
            )
            part = jnp.stack([even, odd], axis=1).reshape(PLANES, 32, 128)
            matrix[other, :, :, pl.ds(128 * pair, 128)] = part.astype(BF16)

    multiply(LEFT, 1, l_all, l_mat, r_matt, TRI, t_send, t_recv)
    fetch(1, l_all, l_mat)

    each_plane(lambda n: arrived(TRI, t_recv, coming_from(n)))
    tri = t_recv[...].astype(F32)
    mean_tri = jnp.sum(tri, axis=0) * (1.0 / C)
    shifted = tri - mean_tri[None]
    scale_tri = lax.rsqrt(jnp.sum(shifted * shifted, axis=0) * (1.0 / C) + EPSILON)
    shift[...] = shifted.reshape(C * 8, 128)
    second = jnp.sum(hid[...].reshape(C, 8, 128) * shifted, axis=0) * (scale_tri * (1.0 / C))
    weight = scale_tri * second

    def grad_step(n):
        plane = going_to(n)
        h = hid[rows(plane), :].reshape(16, 8, 128)
        off = shift[rows(plane), :].reshape(16, 8, 128)
        grad_tri = scale_tri[None] * (h - mean_h[None] - off * weight[None])
        g_send[tiles(plane)] = grad_tri.astype(BF16)
        send_plane(GRAD, n, g_send, g_all.at[core])

    each_plane(grad_step)

    out_bias = column(ob_ref)
    for g in range(GROUPS):
        hat = shift[pl.ds(g, C, stride=8), :] * scale_tri[g : g + 1]
        mixed = nn(owt[...], (hat * out_gain + out_bias).astype(BF16))
        out_gate = gate[g]
        grad_logit = cot_t[g] * mixed * out_gate * (1.0 - out_gate)
        grad_acc[g] = nn(w_ref[:, pl.ds(512, 128)], grad_logit.astype(BF16))

    multiply(GRAD, 2, g_all, gt_mat, r_mat, GRAD_LEFT, gl_send, gl_recv)
    fetch(2, g_all, gt_mat)
    for pair in range(4):
        block = gt_mat[:, :, :, pl.ds(128 * pair, 128)].reshape(N, 128)
        gtt[pl.ds(4 * pair, 4)] = block.T.reshape(4, 32, N)
    mine = gtt[:, pl.ds(pl.multiple_of(16 * core, 16), 16), :].reshape(256, N)
    total = nn(mine, l_mat[...].reshape(N, N))
    for pair in range(4):
        gr_f32[pair] = total[:, 128 * pair : 128 * pair + 128].reshape(2, 8, 16, 128)

    def right_step(step):
        high, low = row_base(step)
        for k in range(2):
            pair = low // 2 + k
            both = swap_halves(
                gr_f32[pair, high, :, pl.ds(0, 8, stride=2), :],
                gr_f32[pair, high, :, pl.ds(1, 8, stride=2), :],
            )
            for e in range(2):
                piece = both[e].astype(BF16)
                for plane in range(PLANES):
                    gr_send[plane * 16 + high * 8 + low + 2 * k + e] = piece[plane]
        send_row(GRAD_RIGHT, step, gr_send, gr_recv)

    each_row(right_step)

    def back(which, buffer, held):
        def step(n):
            plane = coming_from(n)
            arrived(which, buffer, plane)
            stage[held, rows(plane), :] = buffer[tiles(plane)].astype(F32).reshape(128, 128)

        each_plane(step)

    back(GRAD_LEFT, gl_recv, 0)
    for g in range(GROUPS):
        grad = stage[0, pl.ds(g, C, stride=8), :]
        both = jnp.concatenate([grad * left_a[g], grad * left_b[g]], axis=0).astype(BF16)
        grad_acc[g] += nn(w_ref[:, pl.ds(0, 256)], both)

    for which, source in enumerate((r_send, l_send, t_send, g_send, gl_send)):
        sent(which, source)
    for which, buffer in enumerate((r_all, l_all, g_all)):
        to_partner_sent(which, buffer)

    back(GRAD_RIGHT, gr_recv, 1)
    for g in range(GROUPS):
        grad = stage[1, pl.ds(g, C, stride=8), :]
        both = jnp.concatenate([grad * right_a[g], grad * right_b[g]], axis=0).astype(BF16)
        full = (grad_acc[g] + nn(w_ref[:, pl.ds(256, 256)], both)) * in_gain
        hat = normed[g]
        first = jnp.sum(full, axis=0, keepdims=True) * (1.0 / C)
        second = jnp.sum(full * hat, axis=0, keepdims=True) * (1.0 / C)
        grad_pair = sinv[g][:1] * (full - first - hat * second)
        out_ref[pl.ds(g * 128, 128), :] = grad_pair.T.astype(BF16)

    sent(GRAD_RIGHT, gr_send)


def on_device(pair_act, cotangent, in_gain, in_bias, proj_weight, out_gain, out_bias, out_weight):
    pairs = pair_act.shape[0] * pair_act.shape[1]
    operands = (
        pair_act.reshape(pairs, C),
        cotangent.reshape(pairs, C),
        in_gain.reshape(1, C),
        in_bias.reshape(1, C),
        proj_weight,
        out_gain.reshape(1, C),
        out_bias.reshape(1, C),
        out_weight,
    )
    pieces = pltpu.VMEM((C, 8, 128), BF16)
    both = pltpu.VMEM((2, C, 8, 128), BF16)
    kept = pltpu.VMEM((GROUPS, C, 128), F32)
    flat = pltpu.VMEM((C * 8, 128), F32)
    out = pl.pallas_call(
        body,
        out_shape=pltpu.VMEM((pairs, C), BF16),
        in_specs=[pl.BlockSpec(memory_space=pl.ANY)] * 8,
        out_specs=pl.BlockSpec(memory_space=pltpu.VMEM),
        scratch_shapes=[pltpu.VMEM(a.shape, a.dtype) for a in operands] + [
            pltpu.VMEM((5 * C, C), BF16),
            pltpu.VMEM((C, C), BF16),
            pltpu.VMEM((GROUPS, C, 128), BF16),
            kept,
            pltpu.VMEM((GROUPS, 8, 128), F32),
            kept, kept, kept, kept, kept, kept, kept,
            flat, flat,
            pltpu.VMEM((2, C * 8, 128), F32),
            pieces, both, pieces, both, pieces, pieces, pieces, both,
            pieces, pieces, pieces, pieces,
            pltpu.VMEM((4, 16, 32, 128), F32),
            pltpu.VMEM((N, N), BF16),
            pltpu.VMEM((N, N), BF16),
            pltpu.VMEM((2, PLANES, 32, N), BF16),
            pltpu.VMEM((2, PLANES, 32, N), BF16),
            pltpu.VMEM((16, 32, N), BF16),
            pltpu.VMEM((4, 2, 8, 16, 128), F32),
            pltpu.SemaphoreType.DMA((8,)),
            pltpu.SemaphoreType.DMA((6,)),
            pltpu.SemaphoreType.DMA((6, PLANES)),
            pltpu.SemaphoreType.DMA((3,)),
            pltpu.SemaphoreType.DMA((3, PLANES)),
        ],
        compiler_params=pltpu.CompilerParams(
            collective_id=0, has_side_effects=True, vmem_limit_bytes=56 << 20
        ),
    )(*operands)
    return out.reshape(pair_act.shape)


def solution(mesh):
    placed = (P("row", "ch", None), P("row", "ch", None), P(), P(), P(), P(), P(), P())
    return jax.shard_map(
        on_device, mesh=mesh, in_specs=placed, out_specs=P("row", "ch", None), check_vma=False
    )
```

```python
import jax
import jax.numpy as jnp
from jax import lax
from jax.experimental import pallas as pl
from jax.experimental.pallas import tpu as pltpu
from jax.sharding import PartitionSpec as P

EPSILON = 1e-05
MESH = pl.DeviceIdType.MESH
F32 = jnp.float32
BF16 = jnp.bfloat16
C = 128
N = 512
GROUPS = 8
PLANES = 8
FAR = (2, 1, 3, 0)
FAR_PLANES = (4, 3, 5, 2, 6, 1, 7, 0)
FAR_FIRST = (0, 4, 3, 5, 2, 6, 1, 7)
RIGHT, LEFT, TRI, GRAD, GRAD_LEFT, GRAD_RIGHT = range(6)


def nn(a, b):
    return lax.dot_general(a, b, (((1,), (0,)), ((), ())), preferred_element_type=F32)


def swap_halves(a, b):
    axis = a.ndim - 1
    low = lax.broadcasted_iota(jnp.int32, a.shape, axis) < 64
    return (
        jnp.where(low, a, pltpu.roll(b, 64, axis)),
        jnp.where(low, pltpu.roll(a, 64, axis), b),
    )


def column(row_ref):
    return jnp.broadcast_to(row_ref[...], (C, C)).T


def distance(n):
    if isinstance(n, int):
        return FAR_FIRST[n]
    return jnp.where(n == 0, 0, 4 + (n // 2) * (2 * lax.rem(n, 2) - 1))


def body(
    x_hbm, cot_hbm, ig_hbm, ib_hbm, w_hbm, og_hbm, ob_hbm, ow_hbm, out_ref,
    x_ref, cot_ref, ig_ref, ib_ref, w_ref, og_ref, ob_ref, ow_ref,
    wt, owt,
    normal, normed, sinv, left_a, left_b, right_a, right_b, gate, cot_t, grad_acc,
    hid, shift, stage,
    r_send, r_all, l_send, l_all, t_send, t_recv, g_send, g_all,
    gl_send, gl_recv, gr_send, gr_recv,
    r_f32, r_mat, r_matt, l_mat, gt_mat, gtt, gr_f32,
    in_sem, send_sem, recv_sem, core_send, core_recv,
):
    row = lax.axis_index("row")
    ch = lax.axis_index("ch")
    core = lax.rem(row, 2)
    other = 1 - core
    z = lax.rem(row // 2, 8)
    y = (row // 16) * 2 + ch // 4
    x = lax.rem(ch, 4)
    me = z * 16 + (row // 16) * 8 + ch
    partner = (row + 1 - 2 * core, ch)

    loads = [
        pltpu.make_async_copy(source, target, in_sem.at[i])
        for i, (source, target) in enumerate((
            (x_hbm, x_ref), (w_hbm, w_ref), (ig_hbm, ig_ref), (ib_hbm, ib_ref),
            (cot_hbm, cot_ref), (og_hbm, og_ref), (ob_hbm, ob_ref), (ow_hbm, ow_ref),
        ))
    ]
    for load in loads:
        load.start()

    ys = [lax.rem(y + d, 4) for d in FAR]
    xs = [lax.rem(x + d, 4) for d in FAR]
    chips = [(yy // 2, lax.rem(yy, 2) * 4 + xx) for yy in ys for xx in xs]

    def device(plane, chip):
        return ((chip[0] * 8 + plane) * 2 + core, chip[1])

    def slot(plane, chip):
        return plane * 16 + chip[0] * 8 + chip[1]

    def each_plane(step):
        for n in range(PLANES):
            step(n)

    barrier = pltpu.get_barrier_semaphore()
    pl.semaphore_signal(barrier, inc=1, device_id=partner, device_id_type=MESH)

    def greet(n):
        plane = lax.rem(z + distance(n), PLANES)
        for chip in chips[:-1]:
            pl.semaphore_signal(
                barrier, inc=1, device_id=device(plane, chip), device_id_type=MESH
            )

        @pl.when(n > 0)
        def _():
            pl.semaphore_signal(
                barrier, inc=1, device_id=device(plane, chips[-1]), device_id_type=MESH
            )

    each_plane(greet)

    def send_plane(which, n, source, target):
        plane = lax.rem(z + distance(n), PLANES)

        def send(chip):
            pltpu.make_async_remote_copy(
                src_ref=source.at[slot(plane, chip)],
                dst_ref=target.at[me],
                send_sem=send_sem.at[which],
                recv_sem=recv_sem.at[which, z],
                device_id=device(plane, chip),
                device_id_type=MESH,
            ).start()

        for chip in chips[:-1]:
            send(chip)

        @pl.when(n > 0)
        def _():
            send(chips[-1])

        @pl.when(n == 0)
        def _():
            pltpu.make_async_copy(source.at[me], target.at[me], recv_sem.at[which, z]).start()

    zs = [lax.rem(z + d, PLANES) for d in FAR_PLANES]

    def row_base(step):
        yy = lax.rem(y + 2 + ((step + 1) // 2) * (1 - 2 * lax.rem(step, 2)), 4)
        return yy // 2, lax.rem(yy, 2) * 4

    def send_row(which, step, source, target):
        high, low = row_base(step)
        for dx, xx in zip(FAR, xs):
            for dz, plane in zip(FAR_PLANES, zs):
                chip = (high, low + xx)

                def send():
                    pltpu.make_async_remote_copy(
                        src_ref=source.at[slot(plane, chip)],
                        dst_ref=target.at[me],
                        send_sem=send_sem.at[which],
                        recv_sem=recv_sem.at[which, z],
                        device_id=device(plane, chip),
                        device_id_type=MESH,
                    ).start()

                if dx or dz:
                    send()
                else:
                    pl.when(step < 3)(send)

                    @pl.when(step == 3)
                    def _():
                        own = pltpu.make_async_copy(
                            source.at[me], target.at[me], recv_sem.at[which, z]
                        )
                        own.start()

    def each_row(step):
        lax.fori_loop(0, 4, lambda n, carry: (step(n), carry)[1], 0)

    def going_to(n):
        return lax.rem(z + distance(n), PLANES)

    def coming_from(n):
        return lax.rem(z + PLANES - distance(n), PLANES)

    def tiles(plane):
        return pl.ds(pl.multiple_of(plane * 16, 16), 16)

    def arrived(which, target, plane):
        part = target.at[tiles(plane)]
        pltpu.make_async_copy(part, part, recv_sem.at[which, plane]).wait()

    def sent(which, source):
        most = source.at[pl.ds(0, C - 1)]
        pltpu.make_async_copy(most, most, send_sem.at[which]).wait()

    def to_partner(which, buffer, plane):
        part = buffer.at[core, tiles(plane)]
        pltpu.make_async_remote_copy(
            src_ref=part,
            dst_ref=part,
            send_sem=core_send.at[which],
            recv_sem=core_recv.at[which, plane],
            device_id=partner,
            device_id_type=MESH,
        ).start()

    def from_partner(which, buffer, plane):
        part = buffer.at[other, tiles(plane)]
        pltpu.make_async_copy(part, part, core_recv.at[which, plane]).wait()

    def to_partner_sent(which, buffer):
        pltpu.make_async_copy(buffer.at[core], buffer.at[core], core_send.at[which]).wait()

    for load in loads[:4]:
        load.wait()
    wt[...] = w_ref[...].astype(F32).T.astype(BF16)
    in_gain = column(ig_ref)
    in_bias = column(ib_ref)
    for g in range(GROUPS):
        act = x_ref[pl.ds(g * 128, 128), :].astype(F32).T
        shifted = act - jnp.sum(act, axis=0, keepdims=True) * (1.0 / C)
        scale = lax.rsqrt(jnp.sum(shifted * shifted, axis=0, keepdims=True) * (1.0 / C) + EPSILON)
        hat = shifted * scale
        normed[g] = hat
        sinv[g] = jnp.broadcast_to(scale, (8, 128))
        normal[g] = (hat * in_gain + in_bias).astype(BF16)
        projected = nn(wt[pl.ds(256, 256), :], normal[g])
        val, sig = projected[:128], jax.nn.sigmoid(projected[128:])
        factor = sig * val
        right_a[g] = sig
        right_b[g] = factor * (1.0 - sig)
        stage[0, pl.ds(g, C, stride=8), :] = factor
    pl.semaphore_wait(barrier, C)

    def rows(plane):
        return pl.ds(pl.multiple_of(plane * 128, 128), 128)

    def send_left(n):
        plane = going_to(n)
        l_send[tiles(plane)] = stage[1, rows(plane), :].reshape(16, 8, 128).astype(BF16)
        send_plane(LEFT, n, l_send, l_all.at[core])

    def row_tiles(plane, base):
        return pl.ds(pl.multiple_of(plane * 16 + base, 4), 4)

    def row_rows(plane, base):
        return pl.ds(pl.multiple_of((plane * 16 + base) * 8, 32), 32)

    def send_right(n):
        plane = going_to(n)
        r_send[tiles(plane)] = stage[0, rows(plane), :].reshape(16, 8, 128).astype(BF16)
        send_plane(RIGHT, n, r_send, r_all.at[core])

    each_plane(send_right)

    for g in range(GROUPS):
        projected = nn(wt[pl.ds(0, 256), :], normal[g])
        val, sig = projected[:128], jax.nn.sigmoid(projected[128:])
        factor = sig * val
        left_a[g] = sig
        left_b[g] = factor * (1.0 - sig)
        stage[1, pl.ds(g, C, stride=8), :] = factor
    each_plane(send_left)

    for load in loads[4:]:
        load.wait()
    owt[...] = ow_ref[...].astype(F32).T.astype(BF16)
    out_gain = column(og_ref)
    mean_h = []
    for g in range(GROUPS):
        out_gate = jax.nn.sigmoid(nn(wt[pl.ds(512, 128), :], normal[g]))
        cotangent = cot_ref[pl.ds(g * 128, 128), :].astype(F32).T
        grad_mixed = cotangent * out_gate
        gate[g] = out_gate
        cot_t[g] = cotangent
        h = nn(ow_ref[...], grad_mixed.astype(BF16)) * out_gain
        hid[pl.ds(g, C, stride=8), :] = h
        mean_h.append(jnp.sum(h, axis=0, keepdims=True) * (1.0 / C))
    mean_h = jnp.concatenate(mean_h, axis=0)

    def place_right(half, plane):
        got = r_all[half, tiles(plane)].astype(F32).reshape(2, 8, 8, 128)
        for pair in range(4):
            even, odd = swap_halves(got[:, 2 * pair], got[:, 2 * pair + 1])
            for high in range(2):
                at = high * 8 + plane
                r_f32[pair, at, pl.ds(half * 16, 8, stride=2), :] = even[high]
                r_f32[pair, at, pl.ds(half * 16 + 1, 8, stride=2), :] = odd[high]

    def right_here(n):
        plane = coming_from(n)
        arrived(RIGHT, r_all.at[core], plane)
        to_partner(0, r_all, plane)
        place_right(core, plane)

    each_plane(right_here)
    each_plane(lambda n: from_partner(0, r_all, coming_from(n)))
    for pair in range(4):
        got = r_all[other].reshape(PLANES, 2, 8, 8, 128)
        even, odd = swap_halves(
            got[:, :, 2 * pair].astype(F32).reshape(16, 8, 128),
            got[:, :, 2 * pair + 1].astype(F32).reshape(16, 8, 128),
        )
        for at in range(16):
            to = (at % 2) * 8 + at // 2
            r_f32[pair, to, pl.ds(other * 16, 8, stride=2), :] = even[at]
            r_f32[pair, to, pl.ds(other * 16 + 1, 8, stride=2), :] = odd[at]
    for pair in range(4):
        part = r_f32[pair].reshape(N, 128)
        r_mat[:, pl.ds(128 * pair, 128)] = part.astype(BF16)
        r_matt[pl.ds(128 * pair, 128), :] = part.T.astype(BF16)

    def place_pairs(buffer, half, plane, matrix):
        got = buffer[half, tiles(plane)].astype(F32).reshape(2, 8, 8, 128)
        parts = []
        for pair in range(4):
            even, odd = swap_halves(got[:, 2 * pair], got[:, 2 * pair + 1])
            parts.append(
                jnp.concatenate([even.reshape(16, 128), odd.reshape(16, 128)], axis=0).astype(BF16)
            )
        whole = jnp.concatenate(parts, axis=1)
        matrix[half, plane] = whole
        return whole

    def take_pieces(even, odd, buffer, plane):
        out = []
        for pair in range(4):
            out.extend(swap_halves(even(pair), odd(pair)))
        whole = jnp.stack(out, axis=1).reshape(16, 8, 128)
        buffer[tiles(plane)] = whole.astype(BF16)

    def take_rows(value, buffer, plane):
        def part(parity):
            return lambda pair: value[
                16 * parity : 16 * parity + 16, 128 * pair : 128 * pair + 128
            ].reshape(2, 8, 128)

        take_pieces(part(0), part(1), buffer, plane)

    def mirrored(n):
        return n if n < 2 else n + 1 - 2 * (n % 2)

    def multiply(got, link, buffer, matrix, factor, replied, send, target):
        def step(pair, carry):
            steps = (2 * pair, 2 * pair + 1)
            planes = [coming_from(n) for n in steps]
            wholes = []
            for plane in planes:
                arrived(got, buffer.at[core], plane)
                to_partner(link, buffer, plane)
                wholes.append(place_pairs(buffer, core, plane, matrix))
            value = nn(jnp.concatenate(wholes, axis=0), factor[...])
            for i, plane in enumerate(planes):
                take_rows(value[32 * i : 32 * i + 32], send, plane)
                send_plane(replied, mirrored(steps[i]), send, target)
            return carry

        for k in range(PLANES // 2):
            step(k, 0)

    def fetch(link, buffer, matrix):
        each_plane(lambda n: from_partner(link, buffer, coming_from(n)))
        got = buffer[other].reshape(PLANES, 2, 8, 8, 128)
        for pair in range(4):
            even, odd = swap_halves(
                got[:, :, 2 * pair].astype(F32), got[:, :, 2 * pair + 1].astype(F32)
            )
            part = jnp.stack([even, odd], axis=1).reshape(PLANES, 32, 128)
            matrix[other, :, :, pl.ds(128 * pair, 128)] = part.astype(BF16)

    multiply(LEFT, 1, l_all, l_mat, r_matt, TRI, t_send, t_recv)
    fetch(1, l_all, l_mat)

    each_plane(lambda n: arrived(TRI, t_recv, coming_from(n)))
    tri = t_recv[...].astype(F32)
    mean_tri = jnp.sum(tri, axis=0) * (1.0 / C)
    shifted = tri - mean_tri[None]
    scale_tri = lax.rsqrt(jnp.sum(shifted * shifted, axis=0) * (1.0 / C) + EPSILON)
    shift[...] = shifted.reshape(C * 8, 128)
    second = jnp.sum(hid[...].reshape(C, 8, 128) * shifted, axis=0) * (scale_tri * (1.0 / C))
    weight = scale_tri * second

    def grad_step(n):
        plane = going_to(n)
        h = hid[rows(plane), :].reshape(16, 8, 128)
        off = shift[rows(plane), :].reshape(16, 8, 128)
        grad_tri = scale_tri[None] * (h - mean_h[None] - off * weight[None])
        g_send[tiles(plane)] = grad_tri.astype(BF16)
        send_plane(GRAD, n, g_send, g_all.at[core])

    each_plane(grad_step)

    out_bias = column(ob_ref)
    for g in range(GROUPS):
        hat = shift[pl.ds(g, C, stride=8), :] * scale_tri[g : g + 1]
        mixed = nn(owt[...], (hat * out_gain + out_bias).astype(BF16))
        out_gate = gate[g]
        grad_logit = cot_t[g] * mixed * out_gate * (1.0 - out_gate)
        grad_acc[g] = nn(w_ref[:, pl.ds(512, 128)], grad_logit.astype(BF16))

    multiply(GRAD, 2, g_all, gt_mat, r_mat, GRAD_LEFT, gl_send, gl_recv)
    fetch(2, g_all, gt_mat)
    for pair in range(4):
        block = gt_mat[:, :, :, pl.ds(128 * pair, 128)].reshape(N, 128)
        gtt[pl.ds(4 * pair, 4)] = block.T.reshape(4, 32, N)
    mine = gtt[:, pl.ds(pl.multiple_of(16 * core, 16), 16), :].reshape(256, N)
    total = nn(mine, l_mat[...].reshape(N, N))
    for pair in range(4):
        gr_f32[pair] = total[:, 128 * pair : 128 * pair + 128].reshape(2, 8, 16, 128)

    def right_step(step):
        high, low = row_base(step)
        for k in range(2):
            pair = low // 2 + k
            both = swap_halves(
                gr_f32[pair, high, :, pl.ds(0, 8, stride=2), :],
                gr_f32[pair, high, :, pl.ds(1, 8, stride=2), :],
            )
            for e in range(2):
                piece = both[e].astype(BF16)
                for plane in range(PLANES):
                    gr_send[plane * 16 + high * 8 + low + 2 * k + e] = piece[plane]
        send_row(GRAD_RIGHT, step, gr_send, gr_recv)

    each_row(right_step)

    def back(which, buffer, held):
        def step(n):
            plane = coming_from(n)
            arrived(which, buffer, plane)
            stage[held, rows(plane), :] = buffer[tiles(plane)].astype(F32).reshape(128, 128)

        each_plane(step)

    back(GRAD_LEFT, gl_recv, 0)
    for g in range(GROUPS):
        grad = stage[0, pl.ds(g, C, stride=8), :]
        both = jnp.concatenate([grad * left_a[g], grad * left_b[g]], axis=0).astype(BF16)
        grad_acc[g] += nn(w_ref[:, pl.ds(0, 256)], both)

    for which, source in enumerate((r_send, l_send, t_send, g_send, gl_send)):
        sent(which, source)
    for which, buffer in enumerate((r_all, l_all, g_all)):
        to_partner_sent(which, buffer)

    back(GRAD_RIGHT, gr_recv, 1)
    for g in range(GROUPS):
        grad = stage[1, pl.ds(g, C, stride=8), :]
        both = jnp.concatenate([grad * right_a[g], grad * right_b[g]], axis=0).astype(BF16)
        full = (grad_acc[g] + nn(w_ref[:, pl.ds(256, 256)], both)) * in_gain
        hat = normed[g]
        first = jnp.sum(full, axis=0, keepdims=True) * (1.0 / C)
        second = jnp.sum(full * hat, axis=0, keepdims=True) * (1.0 / C)
        grad_pair = sinv[g][:1] * (full - first - hat * second)
        out_ref[pl.ds(g * 128, 128), :] = grad_pair.T.astype(BF16)

    sent(GRAD_RIGHT, gr_send)


def on_device(pair_act, cotangent, in_gain, in_bias, proj_weight, out_gain, out_bias, out_weight):
    pairs = pair_act.shape[0] * pair_act.shape[1]
    operands = (
        pair_act.reshape(pairs, C),
        cotangent.reshape(pairs, C),
        in_gain.reshape(1, C),
        in_bias.reshape(1, C),
        proj_weight,
        out_gain.reshape(1, C),
        out_bias.reshape(1, C),
        out_weight,
    )
    pieces = pltpu.VMEM((C, 8, 128), BF16)
    both = pltpu.VMEM((2, C, 8, 128), BF16)
    kept = pltpu.VMEM((GROUPS, C, 128), F32)
    flat = pltpu.VMEM((C * 8, 128), F32)
    out = pl.pallas_call(
        body,
        out_shape=pltpu.VMEM((pairs, C), BF16),
        in_specs=[pl.BlockSpec(memory_space=pl.ANY)] * 8,
        out_specs=pl.BlockSpec(memory_space=pltpu.VMEM),
        scratch_shapes=[pltpu.VMEM(a.shape, a.dtype) for a in operands] + [
            pltpu.VMEM((5 * C, C), BF16),
            pltpu.VMEM((C, C), BF16),
            pltpu.VMEM((GROUPS, C, 128), BF16),
            kept,
            pltpu.VMEM((GROUPS, 8, 128), F32),
            kept, kept, kept, kept, kept, kept, kept,
            flat, flat,
            pltpu.VMEM((2, C * 8, 128), F32),
            pieces, both, pieces, both, pieces, pieces, pieces, both,
            pieces, pieces, pieces, pieces,
            pltpu.VMEM((4, 16, 32, 128), F32),
            pltpu.VMEM((N, N), BF16),
            pltpu.VMEM((N, N), BF16),
            pltpu.VMEM((2, PLANES, 32, N), BF16),
            pltpu.VMEM((2, PLANES, 32, N), BF16),
            pltpu.VMEM((16, 32, N), BF16),
            pltpu.VMEM((4, 2, 8, 16, 128), F32),
            pltpu.SemaphoreType.DMA((8,)),
            pltpu.SemaphoreType.DMA((6,)),
            pltpu.SemaphoreType.DMA((6, PLANES)),
            pltpu.SemaphoreType.DMA((3,)),
            pltpu.SemaphoreType.DMA((3, PLANES)),
        ],
        compiler_params=pltpu.CompilerParams(
            collective_id=0, has_side_effects=True, vmem_limit_bytes=56 << 20
        ),
    )(*operands)
    return out.reshape(pair_act.shape)


def solution(mesh):
    placed = (P("row", "ch", None), P("row", "ch", None), P(), P(), P(), P(), P(), P())
    return jax.shard_map(
        on_device, mesh=mesh, in_specs=placed, out_specs=P("row", "ch", None), check_vma=False
    )
```
